256 devices in a mesh: row: 16 (over x, z_lo, core), col: 16 (over y, z_hi).
Axes of the slice: x: 4, y: 4, z: 8 (z_hi: 4, z_lo: 2; z = z_hi * 2 + z_lo), core: 2. Of those that a mesh axis runs over, the one named last changes fastest.
Arguments:
- points: float32 [3, 65536], P(None, ('row', 'col')), may hold values from -1 to 1, as said below
- self_term: float32 [65536], P(('row', 'col')), may hold values from 1 to 2
- solution: float32 [128, 65536], P(None, ('row', 'col')), may hold values from -6 to 6
- residual: float32 [128, 65536], P(None, ('row', 'col')), may hold values from -45 to 45
- direction: float32 [128, 65536], P(None, ('row', 'col')), may hold values from -45 to 45
Outputs:
- solution_next: float32 [128, 65536], P(None, ('row', 'col'))
- residual_next: float32 [128, 65536], P(None, ('row', 'col'))
- direction_next: float32 [128, 65536], P(None, ('row', 'col'))
The draws below stay inside these ranges and needn't reach their ends.
Inputs may be any that keep to these rules, and one draw needn't show every extreme that they name: Every column of points is a unit vector.
All inputs are finite; a program needn't handle non-finite values.
Results may differ from the reference program's by a relative error of at most 0.00011.
Values sent between devices are 32-bit elements; how exact they have to be, the bound alone decides.
No kernel may reach another device: no remote copies, remote signals or barrier semaphores. Data moves between devices by JAX's collectives and lax.ppermute only.
A program may use at most 128 MiB of HBM per device.

```python
import math
import jax
import jax.numpy as jnp
from jax import lax

RHS = 128
N = 65536


def draw_points(key, part):
    key = jax.random.fold_in(key, 1)
    height_key, angle_key = jax.random.split(key)
    height = jax.random.uniform(height_key, (N,), jnp.float32, -1.0, 1.0)
    azimuth = jax.random.uniform(angle_key, (N,), jnp.float32, -math.pi, math.pi)
    radial = jnp.sqrt(jnp.maximum(1.0 - height * height, 0.0))
    return jnp.stack([radial * jnp.cos(azimuth), radial * jnp.sin(azimuth), height])


def draw_residual(key, part):
    key = jax.random.fold_in(key, 2)
    noise_key = jax.random.fold_in(key, 0)
    position = jnp.arange(N, dtype=jnp.float32)
    rising = jnp.exp(math.log(3.0) * position / max(N - 1, 1))
    noise = jnp.clip(jax.random.normal(noise_key, (RHS, N), jnp.float32), -4.0, 4.0)
    return noise * rising[None, :]


def draw_direction(key, part):
    key = jax.random.fold_in(key, 3)
    noise_key = jax.random.fold_in(key, 0)
    position = jnp.arange(N, dtype=jnp.float32)
    rising = jnp.exp(math.log(3.0) * position / max(N - 1, 1))
    noise = jnp.clip(jax.random.normal(noise_key, (RHS, N), jnp.float32), -4.0, 4.0)
    return noise * rising[None, :]


def steps_of(stream_key, extent, shards, low, largest):
    level = 1.0
    for dim, shards_of in shards:
        steps = jax.random.uniform(jax.random.fold_in(jax.random.fold_in(stream_key, 6), dim), (shards_of,), jnp.float32, low / len(shards), largest / len(shards))
        level = level * jnp.repeat(jnp.exp(steps), extent[dim] // shards_of).reshape((-1,) + (1,) * (len(extent) - 1 - dim))
    return level


def gaussian(stream_key, dims, spread, reach, cuts=(), kind=jnp.bfloat16):
    values = jax.random.normal(stream_key, dims, jnp.float32) * spread
    if len(cuts) > 0:
        values = steps_of(stream_key, dims, cuts, -0.22, 0.18) * values
    return jnp.clip(values, min=-reach, max=reach).astype(kind)


def setup_inputs(seed: int = 0) -> dict:
    keys = jax.random.split(jax.random.key(seed), 6)
    points = draw_points(jax.random.fold_in(keys[5], 71), 0)
    self_term = jnp.clip(1.0 + 1.0 * jax.random.uniform(keys[1], (N,), jnp.float32) ** steps_of(keys[1], (N,), ((0, 256),), -0.2, 0.2), 1.0, 2.0)
    solution = gaussian(keys[2], (RHS, N), 1.0, 6.0, ((1, 256),), jnp.float32)
    residual = draw_residual(jax.random.fold_in(keys[5], 71), 0)
    direction = draw_direction(jax.random.fold_in(keys[5], 71), 0)
    return dict(points=points, self_term=self_term, solution=solution, residual=residual, direction=direction)


def kernel_apply(points, values):
    total = points.shape[1]
    smoothing = 1.0 / math.sqrt(total)
    block_rows = min(512, total)
    blocks = points.reshape(3, total // block_rows, block_rows).transpose(1, 0, 2)

    def one_block(target):
        squared = (points[0][:, None] - target[0][None, :]) ** 2
        squared = squared + (points[1][:, None] - target[1][None, :]) ** 2
        squared = squared + (points[2][:, None] - target[2][None, :]) ** 2
        kernel = 1.0 / jnp.sqrt(squared + smoothing * smoothing)
        return jnp.dot(values, kernel, precision=lax.Precision.HIGHEST, preferred_element_type=jnp.float32)
    result = lax.map(one_block, blocks)
    return result.transpose(1, 0, 2).reshape(values.shape[0], total)

def reference(points, self_term, solution, residual, direction):
    total = points.shape[1]
    norm_now = lax.optimization_barrier(jnp.sum(residual * residual, axis=1))
    applied = self_term[None, :] * direction + kernel_apply(points, direction) / math.sqrt(total)
    curvature = lax.optimization_barrier(jnp.sum(direction * applied, axis=1))
    step_len = norm_now / (curvature + 1e-06)
    solution_next = solution + step_len[:, None] * direction
    residual_next = residual - step_len[:, None] * applied
    norm_next = lax.optimization_barrier(jnp.sum(residual_next * residual_next, axis=1))
    factor = norm_next / (norm_now + 1e-06)
    direction_next = residual_next + factor[:, None] * direction
    return (solution_next, residual_next, direction_next)
```

```python
import functools
import math

import jax
import jax.numpy as jnp
from jax import lax
from jax.experimental import pallas as pl
from jax.experimental.pallas import tpu as pltpu
from jax.sharding import Mesh, PartitionSpec as P

FINE = ("x", "zl", "c", "y", "zh")
SIZES = (4, 2, 2, 4, 4)
SOURCES = ("x", "y")
RING = ("zl", "zh")
PART = 256
WIDE = 1024
LANES = 256


def operator_kernel(smoothing, target_ref, source_ref, out_ref, target_cols, source_rows, weights, tile_a, tile_b):
    target_blocks, _, block = target_ref.shape
    source_blocks = source_ref.shape[0]
    systems = weights.shape[1] // 2
    for b in range(target_blocks):
        target_cols[b * block : (b + 1) * block, :] = jnp.transpose(target_ref[b])
    for b in range(source_blocks):
        rows = slice(b * block, (b + 1) * block)
        values = jnp.transpose(source_ref[b, :systems, :])
        high = values.astype(jnp.bfloat16)
        weights[rows, :systems] = high
        weights[rows, systems:] = (values - high.astype(jnp.float32)).astype(jnp.bfloat16)
        source_rows[:, rows] = source_ref[b, systems:, :]
    targets = target_blocks * block
    across = source_blocks * block // WIDE
    steps = (targets // PART) * across
    tiles = (tile_a, tile_b)

    def make(step, tile):
        first = pl.multiple_of((step // across) * PART, PART)
        column = pl.multiple_of((step % across) * WIDE, WIDE)
        for r in range(0, PART, 16):
            place = [
                jnp.broadcast_to(target_cols[pl.ds(first + r, 16), i : i + 1], (16, LANES)) for i in range(3)
            ]
            for c in range(0, WIDE, LANES):
                lanes = pl.ds(column + c, LANES)
                dx = source_rows[0:1, lanes] - place[0]
                dy = source_rows[1:2, lanes] - place[1]
                dz = source_rows[2:3, lanes] - place[2]
                kernel = lax.rsqrt(dx * dx + dy * dy + (dz * dz + smoothing * smoothing))
                high = kernel.astype(jnp.bfloat16)
                tile[r : r + 16, c : c + LANES] = high
                tile[PART + r : PART + r + 16, c : c + LANES] = (kernel - high.astype(jnp.float32)).astype(
                    jnp.bfloat16
                )

    def multiply(step, tile):
        rows = pl.ds(pl.multiple_of((step // across) * PART, PART), PART)
        column = pl.multiple_of((step % across) * WIDE, WIDE)
        product = jnp.dot(tile[...], weights[pl.ds(column, WIDE), :], preferred_element_type=jnp.float32)
        out_ref[rows, :] += (product[:PART, :systems] + product[PART:, systems:]) + (
            product[:PART, systems:] + product[PART:, :systems]
        )

    out_ref[...] = jnp.zeros_like(out_ref)
    make(0, tile_a)

    def two_steps(pair, carry):
        for half in range(2):
            step = pair * 2 + half
            make(jnp.minimum(step + 1, steps - 1), tiles[1 - half])
            multiply(step, tiles[half])
        return carry

    lax.fori_loop(0, steps // 2, two_steps, 0)


def apply_operator(targets, sources, smoothing):
    target_blocks, coords, block = targets.shape
    source_blocks, rows, _ = sources.shape
    systems = rows - coords
    return pl.pallas_call(
        functools.partial(operator_kernel, smoothing),
        out_shape=jax.ShapeDtypeStruct((target_blocks * block, systems), jnp.float32),
        in_specs=[pl.BlockSpec(memory_space=pltpu.VMEM)] * 2,
        out_specs=pl.BlockSpec(memory_space=pltpu.VMEM),
        scratch_shapes=[
            pltpu.VMEM((target_blocks * block, coords), jnp.float32),
            pltpu.VMEM((coords, source_blocks * block), jnp.float32),
            pltpu.VMEM((source_blocks * block, 2 * systems), jnp.bfloat16),
            pltpu.VMEM((2 * PART, WIDE), jnp.bfloat16),
            pltpu.VMEM((2 * PART, WIDE), jnp.bfloat16),
        ],
        compiler_params=pltpu.CompilerParams(vmem_limit_bytes=40 * 2**20),
        name="operator",
    )(targets, sources)


def column_sums(values):
    half = values.shape[1] // 2
    return jnp.sum(jnp.transpose(values[:, :half] + values[:, half:]), axis=0, keepdims=True)


def products_kernel(scale, parts_ref, self_ref, residual_ref, direction_ref, applied_ref, sums_ref):
    total = parts_ref[0]
    for part in range(1, parts_ref.shape[0]):
        total = total + parts_ref[part]
    direction = direction_ref[...]
    residual = residual_ref[...]
    applied = self_ref[...] * direction + jnp.transpose(total) * scale
    applied_ref[...] = applied
    sums = jnp.concatenate(
        [
            column_sums(residual * residual),
            column_sums(direction * applied),
            column_sums(residual * applied),
            column_sums(applied * applied),
        ],
        axis=1,
    )
    sums_ref[...] = jnp.broadcast_to(sums[None], sums_ref.shape)


def update_kernel(
    sums_ref, solution_ref, residual_ref, direction_ref, applied_ref, solution_out, residual_out, direction_out
):
    systems = solution_ref.shape[0]
    sums = jnp.sum(sums_ref[...], axis=0)
    norm_now, curvature, cross, image = (sums[:, i * systems : (i + 1) * systems] for i in range(4))
    step_len = norm_now / (curvature + 1e-06)
    norm_next = jnp.maximum(norm_now + step_len * (step_len * image - 2.0 * cross), 0.0)
    factor = norm_next / (norm_now + 1e-06)
    step_len = jnp.transpose(jnp.broadcast_to(step_len, (systems, systems)))
    factor = jnp.transpose(jnp.broadcast_to(factor, (systems, systems)))
    for c in range(0, solution_ref.shape[1], systems):
        cols = slice(c, c + systems)
        direction = direction_ref[:, cols]
        residual_next = residual_ref[:, cols] - step_len * applied_ref[:, cols]
        solution_out[:, cols] = solution_ref[:, cols] + step_len * direction
        residual_out[:, cols] = residual_next
        direction_out[:, cols] = residual_next + factor * direction


def on_device(points, self_term, solution, residual, direction):
    systems, block = direction.shape
    total = block * math.prod(SIZES)
    smoothing = 1.0 / math.sqrt(total)
    vmem = pl.BlockSpec(memory_space=pltpu.VMEM)
    coords = jnp.concatenate([points, jnp.zeros((5, block), jnp.float32)], axis=0)
    cores = ("c",) + RING
    group = lax.axis_size(cores)
    targets = lax.all_to_all(jnp.broadcast_to(coords[None], (group,) + coords.shape), cores, 0, 0)
    mine = jnp.concatenate([direction, coords], axis=0)
    planes = lax.axis_size(SOURCES)
    sources = lax.all_to_all(jnp.broadcast_to(mine[None], (planes,) + mine.shape), SOURCES, 0, 0)
    partial = apply_operator(targets, sources, smoothing)
    halves = partial.reshape(2, group // 2, block, systems)
    core = lax.axis_index("c")
    keep = lax.dynamic_index_in_dim(halves, core, 0, keepdims=False)
    give = lax.dynamic_index_in_dim(halves, 1 - core, 0, keepdims=False)
    keep = keep + lax.ppermute(give, "c", [(0, 1), (1, 0)])
    parts = lax.all_to_all(keep, RING, 0, 0)
    devices = math.prod(SIZES)
    applied, sums = pl.pallas_call(
        functools.partial(products_kernel, 1.0 / math.sqrt(total)),
        out_shape=(
            jax.ShapeDtypeStruct((systems, block), jnp.float32),
            jax.ShapeDtypeStruct((devices, 1, 4 * systems), jnp.float32),
        ),
        in_specs=[vmem] * 4,
        out_specs=(vmem, vmem),
        name="products",
    )(parts, self_term[None, :], residual, direction)
    sums = lax.all_to_all(sums, FINE, 0, 0)
    return pl.pallas_call(
        update_kernel,
        out_shape=(jax.ShapeDtypeStruct((systems, block), jnp.float32),) * 3,
        in_specs=[vmem] * 5,
        out_specs=(vmem,) * 3,
        name="update",
    )(sums, solution, residual, direction, applied)


def solution(mesh):
    fine = Mesh(mesh.devices.reshape(SIZES), FINE)
    matrix = P(None, FINE)
    return jax.shard_map(
        on_device,
        mesh=fine,
        in_specs=(matrix, P(FINE), matrix, matrix, matrix),
        out_specs=(matrix, matrix, matrix),
        check_vma=False,
    )
```

```python
import functools
import math

import jax
import jax.numpy as jnp
from jax import lax
from jax.experimental import pallas as pl
from jax.experimental.pallas import tpu as pltpu
from jax.sharding import Mesh, PartitionSpec as P

FINE = ("x", "zl", "c", "y", "zh")
SIZES = (4, 2, 2, 4, 4)
RING = ("zl", "zh")
PLANE = ("x", "c", "y")
PART = 256
LANES = 256
COORDS = 8
VMEM = pl.BlockSpec(memory_space=pltpu.VMEM)
SMEM = pl.BlockSpec(memory_space=pltpu.SMEM)


def shift(value, axes, by):
    size = lax.axis_size(axes)
    return lax.ppermute(value, axes, [(i, (i + by) % size) for i in range(size)])


def ring_index(z):
    return (z % 2) * SIZES[4] + z // 2


def ring_shift(value, by):
    size = lax.axis_size(RING)
    return lax.ppermute(value, RING, [(ring_index(z), ring_index((z + by) % size)) for z in range(size)])


def prepare(groups, weights, rows):
    systems = weights.shape[0] // 2
    at = 0
    for group in groups:
        for b in range(group.shape[0]):
            block = group.shape[2]
            cols = slice(at, at + block)
            values = group[b, :systems, :]
            high = values.astype(jnp.bfloat16)
            weights[:systems, cols] = high
            weights[systems:, cols] = (values - high.astype(jnp.float32)).astype(jnp.bfloat16)
            for i in range(3):
                rows[8 * i : 8 * i + 8, cols] = jnp.broadcast_to(group[b, systems + i : systems + i + 1, :], (8, block))
            at += block


def accumulate(smoothing, wide, weights, rows, columns, out, tile_a, tile_b):
    systems = out.shape[1]
    across = weights.shape[1] // wide
    steps = (out.shape[0] // PART) * across
    tiles = (tile_a, tile_b)

    def make(step, tile):
        first = pl.multiple_of((step // across) * PART, PART)
        column = pl.multiple_of((step % across) * wide, wide)
        for r in range(0, PART, 16):
            place = [jnp.broadcast_to(columns[pl.ds(first + r, 16), i : i + 1], (16, LANES)) for i in range(3)]
            for c in range(0, wide, LANES):
                lanes = pl.ds(column + c, LANES)
                far = [jnp.concatenate([rows[8 * i : 8 * i + 8, lanes]] * 2, axis=0) for i in range(3)]
                dx, dy, dz = (far[i] - place[i] for i in range(3))
                kernel = lax.rsqrt(dx * dx + dy * dy + (dz * dz + smoothing * smoothing))
                high = kernel.astype(jnp.bfloat16)
                low = (kernel - high.astype(jnp.float32)).astype(jnp.bfloat16)
                tile[r : r + 16, c : c + LANES] = high
                tile[PART + r : PART + r + 16, c : c + LANES] = low

    def multiply(step, tile):
        at = pl.ds(pl.multiple_of((step // across) * PART, PART), PART)
        column = pl.multiple_of((step % across) * wide, wide)
        product = lax.dot_general(
            tile[...],
            weights[:, pl.ds(column, wide)],
            (((1,), (1,)), ((), ())),
            preferred_element_type=jnp.float32,
        )
        out[at, :] += (product[:PART, :systems] + product[PART:, systems:]) + (
            product[:PART, systems:] + product[PART:, :systems]
        )

    make(0, tile_a)

    def two_steps(pair, carry):
        for half in range(2):
            step = pair * 2 + half
            make(jnp.minimum(step + 1, steps - 1), tiles[1 - half])
            multiply(step, tiles[half])
        return carry

    lax.fori_loop(0, steps // 2, two_steps, 0)


def bulk_kernel(smoothing, wide, count, started, *refs):
    groups, refs = refs[:count], refs[count:]
    target, refs = refs[0], refs[1:]
    before, refs = (refs[0], refs[1:]) if started else (None, refs)
    out, weights, rows, columns, tile_a, tile_b = refs
    block = target.shape[2]
    for b in range(target.shape[0]):
        columns[b * block : (b + 1) * block, :] = jnp.transpose(target[b])
    prepare(groups, weights, rows)
    out[...] = before[...] if started else jnp.zeros_like(out)
    accumulate(smoothing, wide, weights, rows, columns, out, tile_a, tile_b)


def step_kernel(smoothing, wide, offset, count, arrived, *refs):
    here, refs = refs[0], refs[1:]
    groups, refs = refs[:count], refs[count:]
    if not count:
        weights, rows, refs = refs[0], refs[1], refs[2:]
    target, before, refs = refs[0], refs[1], refs[2:]
    came, refs = (refs[0], refs[1:]) if arrived else (None, refs)
    out, refs = refs[0], refs[1:]
    if count:
        weights, rows, refs = refs[0], refs[1], refs[2:]
        prepare(groups, weights, rows)
    columns, tile_a, tile_b = refs
    length = target.shape[0]
    z = lax.rem(here[0] + offset, length)
    which = lax.rem(z, 2) * (length // 2) + lax.div(z, 2)
    columns[...] = jnp.transpose(target[which])
    block = out.shape[0]
    earlier = before[pl.ds(pl.multiple_of(which * block, block), block), :]
    out[...] = earlier + came[...] if arrived else earlier
    accumulate(smoothing, wide, weights, rows, columns, out, tile_a, tile_b)


def cost(targets, sources, systems):
    return pl.CostEstimate(
        flops=16 * targets * sources * systems, bytes_accessed=4 * targets * systems, transcendentals=targets * sources
    )


def bulk(groups, targets, before, smoothing, wide=1024):
    ring, coords, block = targets.shape
    systems = groups[0].shape[1] - coords
    sources = sum(g.shape[0] for g in groups) * block
    started = before is not None
    return pl.pallas_call(
        functools.partial(bulk_kernel, smoothing, wide, len(groups), started),
        out_shape=jax.ShapeDtypeStruct((ring * block, systems), jnp.float32),
        in_specs=[VMEM] * (len(groups) + 1 + started),
        out_specs=VMEM,
        scratch_shapes=[
            pltpu.VMEM((2 * systems, sources), jnp.bfloat16),
            pltpu.VMEM((24, sources), jnp.float32),
            pltpu.VMEM((ring * block, coords), jnp.float32),
            pltpu.VMEM((2 * PART, wide), jnp.bfloat16),
            pltpu.VMEM((2 * PART, wide), jnp.bfloat16),
        ],
        compiler_params=pltpu.CompilerParams(vmem_limit_bytes=24 * 2**20),
        cost_estimate=cost(ring * block, sources, systems),
        name="bulk",
    )(*groups, targets, *([before] if started else []))


def ring_step(here, offset, groups, prepared, targets, before, arrived, smoothing, wide=512):
    ring, coords, block = targets.shape
    systems = before.shape[1]
    sources = prepared[0].shape[1] if prepared else sum(g.shape[0] for g in groups) * block
    came = [] if arrived is None else [arrived]
    outs = [jax.ShapeDtypeStruct((block, systems), jnp.float32)]
    if groups:
        outs += [
            jax.ShapeDtypeStruct((2 * systems, sources), jnp.bfloat16),
            jax.ShapeDtypeStruct((24, sources), jnp.float32),
        ]
    operands = [*groups, *prepared, targets, before, *came]
    return pl.pallas_call(
        functools.partial(step_kernel, smoothing, wide, offset % ring, len(groups), bool(came)),
        out_shape=outs,
        in_specs=[SMEM] + [VMEM] * len(operands),
        out_specs=[VMEM] * len(outs),
        scratch_shapes=[
            pltpu.VMEM((block, coords), jnp.float32),
            pltpu.VMEM((2 * PART, wide), jnp.bfloat16),
            pltpu.VMEM((2 * PART, wide), jnp.bfloat16),
        ],
        compiler_params=pltpu.CompilerParams(vmem_limit_bytes=24 * 2**20),
        cost_estimate=cost(block, sources, systems),
        name="ring_step",
    )(here, *operands)


def column_sums(values):
    half = values.shape[1] // 2
    return jnp.sum(jnp.transpose(values[:, :half] + values[:, half:]), axis=0, keepdims=True)


def products_kernel(scale, own, up, down, self_term, residual_ref, direction_ref, applied_ref, sums_ref):
    total = (own[...] + up[...]) + down[...]
    direction = direction_ref[...]
    residual = residual_ref[...]
    applied = self_term[...] * direction + jnp.transpose(total) * scale
    applied_ref[...] = applied
    sums = jnp.concatenate(
        [
            column_sums(residual * residual),
            column_sums(direction * applied),
            column_sums(residual * applied),
            column_sums(applied * applied),
        ],
        axis=1,
    )
    sums_ref[...] = jnp.broadcast_to(sums[None], sums_ref.shape)


def spread_kernel(parts, out):
    out[...] = jnp.broadcast_to(jnp.sum(parts[...], axis=0, keepdims=True), out.shape)


def update_kernel(
    sums_ref, solution_ref, residual_ref, direction_ref, applied_ref, solution_out, residual_out, direction_out
):
    systems = solution_ref.shape[0]
    sums = jnp.sum(sums_ref[...], axis=0)
    norm_now, curvature, cross, image = (sums[:, i * systems : (i + 1) * systems] for i in range(4))
    step_len = norm_now / (curvature + 1e-06)
    norm_next = jnp.maximum(norm_now + step_len * (step_len * image - 2.0 * cross), 0.0)
    factor = norm_next / (norm_now + 1e-06)
    step_len = jnp.transpose(jnp.broadcast_to(step_len, (systems, systems)))
    factor = jnp.transpose(jnp.broadcast_to(factor, (systems, systems)))
    for c in range(0, solution_ref.shape[1], systems):
        cols = slice(c, c + systems)
        direction = direction_ref[:, cols]
        residual_next = residual_ref[:, cols] - step_len * applied_ref[:, cols]
        solution_out[:, cols] = solution_ref[:, cols] + step_len * direction
        residual_out[:, cols] = residual_next
        direction_out[:, cols] = residual_next + factor * direction


def on_device(points, self_term, solution, residual, direction):
    systems, block = direction.shape
    total = block * math.prod(SIZES)
    smoothing = 1.0 / math.sqrt(total)
    ring = lax.axis_size(RING)
    here = jnp.reshape(lax.axis_index("zh") * 2 + lax.axis_index("zl"), (1,))
    small = pltpu.CompilerParams(vmem_limit_bytes=16 * 2**20)

    mine = jnp.concatenate([direction, points, jnp.zeros((COORDS - 3, block), jnp.float32)], axis=0)
    coords = jnp.concatenate([points, jnp.zeros((COORDS - 3, block), jnp.float32)], axis=0)
    line = jnp.stack([mine, shift(mine, "x", 1), shift(mine, "x", -1), shift(mine, "x", 2)])
    targets = lax.all_to_all(jnp.broadcast_to(coords[None], (ring,) + coords.shape), RING, 0, 0)
    above, below = shift(line, "y", 1), shift(line, "y", -1)
    sums = bulk([line, shift(line, "c", 1)], targets, None, smoothing)
    sums, above, below = lax.optimization_barrier((sums, above, below))
    far = [shift(above[:2], "y", 1), shift(below[2:], "y", -1)]
    sums = bulk([above, shift(above, "c", 1)], targets, sums, smoothing)
    last = [below, *far]
    last += [shift(part, "c", 1) for part in last]

    up, *prepared = ring_step(here, 4, last, [], targets, sums, None, smoothing)
    up = ring_shift(up, 1)
    (down,) = ring_step(here, -3, [], prepared, targets, sums, None, smoothing)
    down = ring_shift(down, -1)
    for away in (3, 2, 1):
        (up,) = ring_step(here, away, [], prepared, targets, sums, up, smoothing)
        up = ring_shift(up, 1)
        if away > 1:
            (down,) = ring_step(here, 1 - away, [], prepared, targets, sums, down, smoothing)
            down = ring_shift(down, -1)
    (own,) = ring_step(here, 0, [], prepared, targets, sums, None, smoothing)

    applied, shares = pl.pallas_call(
        functools.partial(products_kernel, 1.0 / math.sqrt(total)),
        out_shape=(
            jax.ShapeDtypeStruct((systems, block), jnp.float32),
            jax.ShapeDtypeStruct((lax.axis_size(PLANE), 1, 4 * systems), jnp.float32),
        ),
        in_specs=[VMEM] * 6,
        out_specs=(VMEM, VMEM),
        compiler_params=small,
        name="products",
    )(own, up, down, self_term[None, :], residual, direction)
    shares = pl.pallas_call(
        spread_kernel,
        out_shape=jax.ShapeDtypeStruct((ring, 1, 4 * systems), jnp.float32),
        in_specs=[VMEM],
        out_specs=VMEM,
        compiler_params=small,
        name="spread",
    )(lax.all_to_all(shares, PLANE, 0, 0))
    return pl.pallas_call(
        update_kernel,
        out_shape=(jax.ShapeDtypeStruct((systems, block), jnp.float32),) * 3,
        in_specs=[VMEM] * 5,
        out_specs=(VMEM,) * 3,
        compiler_params=small,
        name="update",
    )(lax.all_to_all(shares, RING, 0, 0), solution, residual, direction, applied)


def solution(mesh):
    fine = Mesh(mesh.devices.reshape(SIZES), FINE)
    matrix = P(None, FINE)
    return jax.shard_map(
        on_device,
        mesh=fine,
        in_specs=(matrix, P(FINE), matrix, matrix, matrix),
        out_specs=(matrix, matrix, matrix),
        check_vma=False,
    )
```

```python
import functools
import math

import jax
import jax.numpy as jnp
from jax import lax
from jax.experimental import pallas as pl
from jax.experimental.pallas import tpu as pltpu
from jax.sharding import Mesh, PartitionSpec as P

FINE = ("x", "zl", "c", "y", "zh")
SIZES = (4, 2, 2, 4, 4)
RING = ("zl", "zh")
PLANE = ("x", "c", "y")
PART = 256
LANES = 256
COORDS = 8
VMEM = pl.BlockSpec(memory_space=pltpu.VMEM)
SMEM = pl.BlockSpec(memory_space=pltpu.SMEM)


def shift(value, axes, by):
    size = lax.axis_size(axes)
    return lax.ppermute(value, axes, [(i, (i + by) % size) for i in range(size)])


def ring_index(z):
    return (z % 2) * SIZES[4] + z // 2


def ring_shift(value, by):
    size = lax.axis_size(RING)
    return lax.ppermute(value, RING, [(ring_index(z), ring_index((z + by) % size)) for z in range(size)])


def pack_kernel(points, direction, mine, coords):
    systems = direction.shape[0]
    mine[...] = jnp.zeros_like(mine)
    mine[:systems, :] = direction[...]
    mine[systems : systems + 3, :] = points[...]
    coords[...] = jnp.broadcast_to(mine[systems:, :][None], coords.shape)


def prepare(groups, weights, rows):
    systems = weights.shape[0] // 2
    at = 0
    for group in groups:
        for b in range(group.shape[0]):
            block = group.shape[2]
            cols = slice(at, at + block)
            values = group[b, :systems, :]
            high = values.astype(jnp.bfloat16)
            weights[:systems, cols] = high
            weights[systems:, cols] = (values - high.astype(jnp.float32)).astype(jnp.bfloat16)
            for i in range(3):
                rows[8 * i : 8 * i + 8, cols] = jnp.broadcast_to(group[b, systems + i : systems + i + 1, :], (8, block))
            at += block


def accumulate(smoothing, wide, weights, rows, columns, out, tile_a, tile_b):
    systems = out.shape[1]
    across = weights.shape[1] // wide
    steps = (out.shape[0] // PART) * across
    tiles = (tile_a, tile_b)

    def make(step, tile):
        first = pl.multiple_of((step // across) * PART, PART)
        column = pl.multiple_of((step % across) * wide, wide)
        for r in range(0, PART, 16):
            place = [jnp.broadcast_to(columns[pl.ds(first + r, 16), i : i + 1], (16, LANES)) for i in range(3)]
            for c in range(0, wide, LANES):
                lanes = pl.ds(column + c, LANES)
                far = [jnp.concatenate([rows[8 * i : 8 * i + 8, lanes]] * 2, axis=0) for i in range(3)]
                dx, dy, dz = (far[i] - place[i] for i in range(3))
                kernel = lax.rsqrt(dx * dx + dy * dy + (dz * dz + smoothing * smoothing))
                high = kernel.astype(jnp.bfloat16)
                low = (kernel - high.astype(jnp.float32)).astype(jnp.bfloat16)
                tile[r : r + 16, c : c + LANES] = high
                tile[PART + r : PART + r + 16, c : c + LANES] = low

    def multiply(step, tile):
        at = pl.ds(pl.multiple_of((step // across) * PART, PART), PART)
        column = pl.multiple_of((step % across) * wide, wide)
        product = lax.dot_general(
            tile[...],
            weights[:, pl.ds(column, wide)],
            (((1,), (1,)), ((), ())),
            preferred_element_type=jnp.float32,
        )
        out[at, :] += (product[:PART, :systems] + product[PART:, systems:]) + (
            product[:PART, systems:] + product[PART:, :systems]
        )

    make(0, tile_a)

    def two_steps(pair, carry):
        for half in range(2):
            step = pair * 2 + half
            make(jnp.minimum(step + 1, steps - 1), tiles[1 - half])
            multiply(step, tiles[half])
        return carry

    lax.fori_loop(0, steps // 2, two_steps, 0)


def bulk_kernel(smoothing, wide, count, started, *refs):
    groups, refs = refs[:count], refs[count:]
    target, refs = refs[0], refs[1:]
    before, refs = (refs[0], refs[1:]) if started else (None, refs)
    out, weights, rows, columns, tile_a, tile_b = refs
    block = target.shape[2]
    for b in range(target.shape[0]):
        columns[b * block : (b + 1) * block, :] = jnp.transpose(target[b])
    prepare(groups, weights, rows)
    out[...] = before[...] if started else jnp.zeros_like(out)
    accumulate(smoothing, wide, weights, rows, columns, out, tile_a, tile_b)


def step_kernel(smoothing, wide, offset, count, arrived, *refs):
    here, refs = refs[0], refs[1:]
    groups, refs = refs[:count], refs[count:]
    if not count:
        weights, rows, refs = refs[0], refs[1], refs[2:]
    target, before, refs = refs[0], refs[1], refs[2:]
    came, refs = (refs[0], refs[1:]) if arrived else (None, refs)
    out, refs = refs[0], refs[1:]
    if count:
        weights, rows, refs = refs[0], refs[1], refs[2:]
        prepare(groups, weights, rows)
    columns, tile_a, tile_b = refs
    length = target.shape[0]
    z = lax.rem(here[0] + offset, length)
    which = lax.rem(z, 2) * (length // 2) + lax.div(z, 2)
    columns[...] = jnp.transpose(target[which])
    block = out.shape[0]
    earlier = before[pl.ds(pl.multiple_of(which * block, block), block), :]
    out[...] = earlier + came[...] if arrived else earlier
    accumulate(smoothing, wide, weights, rows, columns, out, tile_a, tile_b)


def cost(targets, sources, systems):
    return pl.CostEstimate(
        flops=16 * targets * sources * systems, bytes_accessed=4 * targets * systems, transcendentals=targets * sources
    )


def bulk(groups, targets, before, smoothing, wide=1024):
    ring, coords, block = targets.shape
    systems = groups[0].shape[1] - coords
    sources = sum(g.shape[0] for g in groups) * block
    started = before is not None
    return pl.pallas_call(
        functools.partial(bulk_kernel, smoothing, wide, len(groups), started),
        out_shape=jax.ShapeDtypeStruct((ring * block, systems), jnp.float32),
        in_specs=[VMEM] * (len(groups) + 1 + started),
        out_specs=VMEM,
        scratch_shapes=[
            pltpu.VMEM((2 * systems, sources), jnp.bfloat16),
            pltpu.VMEM((24, sources), jnp.float32),
            pltpu.VMEM((ring * block, coords), jnp.float32),
            pltpu.VMEM((2 * PART, wide), jnp.bfloat16),
            pltpu.VMEM((2 * PART, wide), jnp.bfloat16),
        ],
        compiler_params=pltpu.CompilerParams(vmem_limit_bytes=24 * 2**20),
        cost_estimate=cost(ring * block, sources, systems),
        name="bulk",
    )(*groups, targets, *([before] if started else []))


def ring_step(here, offset, groups, prepared, targets, before, arrived, smoothing, wide=512):
    ring, coords, block = targets.shape
    systems = before.shape[1]
    sources = prepared[0].shape[1] if prepared else sum(g.shape[0] for g in groups) * block
    came = [] if arrived is None else [arrived]
    outs = [jax.ShapeDtypeStruct((block, systems), jnp.float32)]
    if groups:
        outs += [
            jax.ShapeDtypeStruct((2 * systems, sources), jnp.bfloat16),
            jax.ShapeDtypeStruct((24, sources), jnp.float32),
        ]
    operands = [*groups, *prepared, targets, before, *came]
    return pl.pallas_call(
        functools.partial(step_kernel, smoothing, wide, offset % ring, len(groups), bool(came)),
        out_shape=outs,
        in_specs=[SMEM] + [VMEM] * len(operands),
        out_specs=[VMEM] * len(outs),
        scratch_shapes=[
            pltpu.VMEM((block, coords), jnp.float32),
            pltpu.VMEM((2 * PART, wide), jnp.bfloat16),
            pltpu.VMEM((2 * PART, wide), jnp.bfloat16),
        ],
        compiler_params=pltpu.CompilerParams(vmem_limit_bytes=24 * 2**20),
        cost_estimate=cost(block, sources, systems),
        name="ring_step",
    )(here, *operands)


def column_sums(values):
    half = values.shape[1] // 2
    return jnp.sum(jnp.transpose(values[:, :half] + values[:, half:]), axis=0, keepdims=True)


def products_kernel(scale, own, up, down, self_term, residual_ref, direction_ref, applied_ref, sums_ref):
    total = (own[...] + up[...]) + down[...]
    direction = direction_ref[...]
    residual = residual_ref[...]
    applied = self_term[...] * direction + jnp.transpose(total) * scale
    applied_ref[...] = applied
    sums = jnp.concatenate(
        [
            column_sums(residual * residual),
            column_sums(direction * applied),
            column_sums(residual * applied),
            column_sums(applied * applied),
        ],
        axis=1,
    )
    sums_ref[...] = jnp.broadcast_to(sums[None], sums_ref.shape)


def spread_kernel(parts, out):
    out[...] = jnp.broadcast_to(jnp.sum(parts[...], axis=0, keepdims=True), out.shape)


def update_kernel(
    sums_ref, solution_ref, residual_ref, direction_ref, applied_ref, solution_out, residual_out, direction_out
):
    systems = solution_ref.shape[0]
    sums = jnp.sum(sums_ref[...], axis=0)
    norm_now, curvature, cross, image = (sums[:, i * systems : (i + 1) * systems] for i in range(4))
    step_len = norm_now / (curvature + 1e-06)
    norm_next = jnp.maximum(norm_now + step_len * (step_len * image - 2.0 * cross), 0.0)
    factor = norm_next / (norm_now + 1e-06)
    step_len = jnp.transpose(jnp.broadcast_to(step_len, (systems, systems)))
    factor = jnp.transpose(jnp.broadcast_to(factor, (systems, systems)))
    for c in range(0, solution_ref.shape[1], systems):
        cols = slice(c, c + systems)
        direction = direction_ref[:, cols]
        residual_next = residual_ref[:, cols] - step_len * applied_ref[:, cols]
        solution_out[:, cols] = solution_ref[:, cols] + step_len * direction
        residual_out[:, cols] = residual_next
        direction_out[:, cols] = residual_next + factor * direction


def on_device(points, self_term, solution, residual, direction):
    systems, block = direction.shape
    total = block * math.prod(SIZES)
    smoothing = 1.0 / math.sqrt(total)
    ring = lax.axis_size(RING)
    here = jnp.reshape(lax.axis_index("zh") * 2 + lax.axis_index("zl"), (1,))
    small = pltpu.CompilerParams(vmem_limit_bytes=16 * 2**20)

    mine, coords = pl.pallas_call(
        pack_kernel,
        out_shape=(
            jax.ShapeDtypeStruct((systems + COORDS, block), jnp.float32),
            jax.ShapeDtypeStruct((ring, COORDS, block), jnp.float32),
        ),
        in_specs=[VMEM] * 2,
        out_specs=(VMEM, VMEM),
        compiler_params=small,
        name="pack",
    )(points, direction)
    targets = lax.all_to_all(coords, RING, 0, 0)
    near = [shift(mine, "x", 1), shift(mine, "x", -1), shift(mine, "x", 2)]
    targets, *near = lax.optimization_barrier((targets, *near))
    line = jnp.stack([mine, *near])
    above, below = shift(line, "y", 1), shift(line, "y", -1)
    sums = bulk([line, shift(line, "c", 1)], targets, None, smoothing)
    sums, above, below = lax.optimization_barrier((sums, above, below))
    far = [shift(above[:2], "y", 1), shift(below[2:], "y", -1)]
    copies = [shift(above, "c", 1), shift(below, "c", 1)]
    sums = bulk([above, below], targets, sums, smoothing)
    sums, *far = lax.optimization_barrier((sums, *far))
    last = copies + far + [shift(part, "c", 1) for part in far]

    up, *prepared = ring_step(here, 4, last, [], targets, sums, None, smoothing)
    up = ring_shift(up, 1)
    (down,) = ring_step(here, -3, [], prepared, targets, sums, None, smoothing)
    down = ring_shift(down, -1)
    for away in (3, 2, 1):
        (up,) = ring_step(here, away, [], prepared, targets, sums, up, smoothing)
        up = ring_shift(up, 1)
        if away > 1:
            (down,) = ring_step(here, 1 - away, [], prepared, targets, sums, down, smoothing)
            down = ring_shift(down, -1)
    (own,) = ring_step(here, 0, [], prepared, targets, sums, None, smoothing)

    applied, shares = pl.pallas_call(
        functools.partial(products_kernel, 1.0 / math.sqrt(total)),
        out_shape=(
            jax.ShapeDtypeStruct((systems, block), jnp.float32),
            jax.ShapeDtypeStruct((lax.axis_size(PLANE), 1, 4 * systems), jnp.float32),
        ),
        in_specs=[VMEM] * 6,
        out_specs=(VMEM, VMEM),
        compiler_params=small,
        name="products",
    )(own, up, down, self_term[None, :], residual, direction)
    shares = pl.pallas_call(
        spread_kernel,
        out_shape=jax.ShapeDtypeStruct((ring, 1, 4 * systems), jnp.float32),
        in_specs=[VMEM],
        out_specs=VMEM,
        compiler_params=small,
        name="spread",
    )(lax.all_to_all(shares, PLANE, 0, 0))
    return pl.pallas_call(
        update_kernel,
        out_shape=(jax.ShapeDtypeStruct((systems, block), jnp.float32),) * 3,
        in_specs=[VMEM] * 5,
        out_specs=(VMEM,) * 3,
        compiler_params=small,
        name="update",
    )(lax.all_to_all(shares, RING, 0, 0), solution, residual, direction, applied)


def solution(mesh):
    fine = Mesh(mesh.devices.reshape(SIZES), FINE)
    matrix = P(None, FINE)
    return jax.shard_map(
        on_device,
        mesh=fine,
        in_specs=(matrix, P(FINE), matrix, matrix, matrix),
        out_specs=(matrix, matrix, matrix),
        check_vma=False,
    )
```

```python
import functools
import math

import jax
import jax.numpy as jnp
from jax import lax
from jax.experimental import pallas as pl
from jax.experimental.pallas import tpu as pltpu
from jax.sharding import Mesh, PartitionSpec as P

FINE = ("x", "zl", "c", "y", "zh")
SIZES = (4, 2, 2, 4, 4)
RING = ("zl", "zh")
TARGETS = ("zl", "c", "zh")
PLANE = ("x", "c", "y")
PART = 256
LANES = 256
COORDS = 8
VMEM = pl.BlockSpec(memory_space=pltpu.VMEM)
SMEM = pl.BlockSpec(memory_space=pltpu.SMEM)


def shift(value, axes, by):
    size = lax.axis_size(axes)
    return lax.ppermute(value, axes, [(i, (i + by) % size) for i in range(size)])


def ring_index(z):
    return (z % 2) * SIZES[4] + z // 2


def ring_shift(value, by):
    size = lax.axis_size(RING)
    return lax.ppermute(value, RING, [(ring_index(z), ring_index((z + by) % size)) for z in range(size)])


def pack_kernel(points, direction, mine, coords):
    systems = direction.shape[0]
    mine[...] = jnp.zeros_like(mine)
    mine[:systems, :] = direction[...]
    mine[systems : systems + 3, :] = points[...]
    coords[...] = jnp.broadcast_to(mine[systems:, :][None], coords.shape)


def prepare(groups, weights, rows):
    systems = weights.shape[0] // 2
    at = 0
    for group in groups:
        for b in range(group.shape[0]):
            block = group.shape[2]
            cols = slice(at, at + block)
            values = group[b, :systems, :]
            high = values.astype(jnp.bfloat16)
            weights[:systems, cols] = high
            weights[systems:, cols] = (values - high.astype(jnp.float32)).astype(jnp.bfloat16)
            for i in range(3):
                rows[8 * i : 8 * i + 8, cols] = jnp.broadcast_to(group[b, systems + i : systems + i + 1, :], (8, block))
            at += block


def accumulate(smoothing, wide, weights, rows, columns, out, tile_a, tile_b):
    systems = out.shape[1]
    across = weights.shape[1] // wide
    steps = (out.shape[0] // PART) * across
    tiles = (tile_a, tile_b)

    def make(step, tile):
        first = pl.multiple_of((step // across) * PART, PART)
        column = pl.multiple_of((step % across) * wide, wide)
        for r in range(0, PART, 16):
            place = [jnp.broadcast_to(columns[pl.ds(first + r, 16), i : i + 1], (16, LANES)) for i in range(3)]
            for c in range(0, wide, LANES):
                lanes = pl.ds(column + c, LANES)
                far = [jnp.concatenate([rows[8 * i : 8 * i + 8, lanes]] * 2, axis=0) for i in range(3)]
                dx, dy, dz = (far[i] - place[i] for i in range(3))
                kernel = lax.rsqrt(dx * dx + dy * dy + (dz * dz + smoothing * smoothing))
                high = kernel.astype(jnp.bfloat16)
                low = (kernel - high.astype(jnp.float32)).astype(jnp.bfloat16)
                tile[r : r + 16, c : c + LANES] = high
                tile[PART + r : PART + r + 16, c : c + LANES] = low

    def multiply(step, tile):
        at = pl.ds(pl.multiple_of((step // across) * PART, PART), PART)
        column = pl.multiple_of((step % across) * wide, wide)
        product = lax.dot_general(
            tile[...],
            weights[:, pl.ds(column, wide)],
            (((1,), (1,)), ((), ())),
            preferred_element_type=jnp.float32,
        )
        out[at, :] += (product[:PART, :systems] + product[PART:, systems:]) + (
            product[:PART, systems:] + product[PART:, :systems]
        )

    make(0, tile_a)

    def two_steps(pair, carry):
        for half in range(2):
            step = pair * 2 + half
            make(jnp.minimum(step + 1, steps - 1), tiles[1 - half])
            multiply(step, tiles[half])
        return carry

    lax.fori_loop(0, steps // 2, two_steps, 0)


def bulk_kernel(smoothing, wide, count, started, *refs):
    groups, refs = refs[:count], refs[count:]
    target, refs = refs[0], refs[1:]
    before, refs = (refs[0], refs[1:]) if started else (None, refs)
    out, weights, rows, columns, tile_a, tile_b = refs
    block = target.shape[2]
    for b in range(target.shape[0]):
        columns[b * block : (b + 1) * block, :] = jnp.transpose(target[b])
    prepare(groups, weights, rows)
    out[...] = before[...] if started else jnp.zeros_like(out)
    accumulate(smoothing, wide, weights, rows, columns, out, tile_a, tile_b)


def step_kernel(smoothing, wide, offset, count, arrived, *refs):
    here, refs = refs[0], refs[1:]
    groups, refs = refs[:count], refs[count:]
    if not count:
        weights, rows, refs = refs[0], refs[1], refs[2:]
    target, before, refs = refs[0], refs[1], refs[2:]
    came, refs = (refs[0], refs[1:]) if arrived else (None, refs)
    out, refs = refs[0], refs[1:]
    if count:
        weights, rows, refs = refs[0], refs[1], refs[2:]
        prepare(groups, weights, rows)
    columns, tile_a, tile_b = refs
    chips = target.shape[0] // 2
    z = lax.rem(here[0] + offset, chips)
    block = target.shape[2]
    for core in range(2):
        which = lax.rem(z, 2) * chips + core * (chips // 2) + lax.div(z, 2)
        rows_of_core = slice(core * block, (core + 1) * block)
        columns[rows_of_core, :] = jnp.transpose(target[which])
        earlier = before[pl.ds(pl.multiple_of(which * block, block), block), :]
        out[rows_of_core, :] = earlier + came[rows_of_core, :] if arrived else earlier
    accumulate(smoothing, wide, weights, rows, columns, out, tile_a, tile_b)


def cost(targets, sources, systems):
    return pl.CostEstimate(
        flops=16 * targets * sources * systems, bytes_accessed=4 * targets * systems, transcendentals=targets * sources
    )


def bulk(groups, targets, before, smoothing, wide=1792):
    ring, coords, block = targets.shape
    systems = groups[0].shape[1] - coords
    sources = sum(g.shape[0] for g in groups) * block
    started = before is not None
    return pl.pallas_call(
        functools.partial(bulk_kernel, smoothing, wide, len(groups), started),
        out_shape=jax.ShapeDtypeStruct((ring * block, systems), jnp.float32),
        in_specs=[VMEM] * (len(groups) + 1 + started),
        out_specs=VMEM,
        scratch_shapes=[
            pltpu.VMEM((2 * systems, sources), jnp.bfloat16),
            pltpu.VMEM((24, sources), jnp.float32),
            pltpu.VMEM((ring * block, coords), jnp.float32),
            pltpu.VMEM((2 * PART, wide), jnp.bfloat16),
            pltpu.VMEM((2 * PART, wide), jnp.bfloat16),
        ],
        compiler_params=pltpu.CompilerParams(vmem_limit_bytes=24 * 2**20),
        cost_estimate=cost(ring * block, sources, systems),
        name="bulk",
    )(*groups, targets, *([before] if started else []))


def ring_step(here, offset, groups, prepared, targets, before, arrived, smoothing, wide=768):
    shards, coords, block = targets.shape
    systems = before.shape[1]
    sources = prepared[0].shape[1] if prepared else sum(g.shape[0] for g in groups) * block
    came = [] if arrived is None else [arrived]
    outs = [jax.ShapeDtypeStruct((2 * block, systems), jnp.float32)]
    if groups:
        outs += [
            jax.ShapeDtypeStruct((2 * systems, sources), jnp.bfloat16),
            jax.ShapeDtypeStruct((24, sources), jnp.float32),
        ]
    operands = [*groups, *prepared, targets, before, *came]
    return pl.pallas_call(
        functools.partial(step_kernel, smoothing, wide, offset % (shards // 2), len(groups), bool(came)),
        out_shape=outs,
        in_specs=[SMEM] + [VMEM] * len(operands),
        out_specs=[VMEM] * len(outs),
        scratch_shapes=[
            pltpu.VMEM((2 * block, coords), jnp.float32),
            pltpu.VMEM((2 * PART, wide), jnp.bfloat16),
            pltpu.VMEM((2 * PART, wide), jnp.bfloat16),
        ],
        compiler_params=pltpu.CompilerParams(vmem_limit_bytes=24 * 2**20),
        cost_estimate=cost(2 * block, sources, systems),
        name="ring_step",
    )(here, *operands)


def column_sums(values):
    half = values.shape[1] // 2
    return jnp.sum(jnp.transpose(values[:, :half] + values[:, half:]), axis=0, keepdims=True)


def merge_kernel(here, own, up, down, keep, give):
    block = keep.shape[0]
    for out, core in ((keep, here[1]), (give, 1 - here[1])):
        at = pl.ds(pl.multiple_of(core * block, block), block)
        out[...] = (own[at, :] + up[at, :]) + down[at, :]


def products_kernel(scale, kept, got, self_term, residual_ref, direction_ref, applied_ref, sums_ref):
    total = kept[...] + got[...]
    direction = direction_ref[...]
    residual = residual_ref[...]
    applied = self_term[...] * direction + jnp.transpose(total) * scale
    applied_ref[...] = applied
    sums = jnp.concatenate(
        [
            column_sums(residual * residual),
            column_sums(direction * applied),
            column_sums(residual * applied),
            column_sums(applied * applied),
        ],
        axis=1,
    )
    sums_ref[...] = jnp.broadcast_to(sums[None], sums_ref.shape)


def spread_kernel(parts, out):
    out[...] = jnp.broadcast_to(jnp.sum(parts[...], axis=0, keepdims=True), out.shape)


def update_kernel(
    sums_ref, solution_ref, residual_ref, direction_ref, applied_ref, solution_out, residual_out, direction_out
):
    systems = solution_ref.shape[0]
    sums = jnp.sum(sums_ref[...], axis=0)
    norm_now, curvature, cross, image = (sums[:, i * systems : (i + 1) * systems] for i in range(4))
    step_len = norm_now / (curvature + 1e-06)
    norm_next = jnp.maximum(norm_now + step_len * (step_len * image - 2.0 * cross), 0.0)
    factor = norm_next / (norm_now + 1e-06)
    step_len = jnp.transpose(jnp.broadcast_to(step_len, (systems, systems)))
    factor = jnp.transpose(jnp.broadcast_to(factor, (systems, systems)))
    for c in range(0, solution_ref.shape[1], systems):
        cols = slice(c, c + systems)
        direction = direction_ref[:, cols]
        residual_next = residual_ref[:, cols] - step_len * applied_ref[:, cols]
        solution_out[:, cols] = solution_ref[:, cols] + step_len * direction
        residual_out[:, cols] = residual_next
        direction_out[:, cols] = residual_next + factor * direction


def on_device(points, self_term, solution, residual, direction):
    systems, block = direction.shape
    total = block * math.prod(SIZES)
    smoothing = 1.0 / math.sqrt(total)
    ring = lax.axis_size(RING)
    here = jnp.stack([lax.axis_index("zh") * 2 + lax.axis_index("zl"), lax.axis_index("c")])
    small = pltpu.CompilerParams(vmem_limit_bytes=16 * 2**20)

    mine, coords = pl.pallas_call(
        pack_kernel,
        out_shape=(
            jax.ShapeDtypeStruct((systems + COORDS, block), jnp.float32),
            jax.ShapeDtypeStruct((2 * ring, COORDS, block), jnp.float32),
        ),
        in_specs=[VMEM] * 2,
        out_specs=(VMEM, VMEM),
        compiler_params=small,
        name="pack",
    )(points, direction)
    targets = lax.all_to_all(coords, TARGETS, 0, 0)
    line = [shift(mine, "x", by) for by in (1, -1, 2)]
    column = [shift(mine, "y", by) for by in (1, -1, 2)]
    targets, *cross = lax.optimization_barrier((targets, *line, *column))
    line, column = jnp.stack(cross[:3]), cross[3:]
    rest = [shift(line, "y", 1), shift(line, "y", -1)] + [shift(column[2][None], "x", by) for by in (1, -1, 2)]
    sums = bulk([mine[None], line] + [part[None] for part in column], targets, None, smoothing)
    sums, *rest = lax.optimization_barrier((sums, *rest))

    up, *prepared = ring_step(here, 4, rest, [], targets, sums, None, smoothing)
    up = ring_shift(up, 1)
    (down,) = ring_step(here, -3, [], prepared, targets, sums, None, smoothing)
    down = ring_shift(down, -1)
    for away in (3, 2, 1):
        (up,) = ring_step(here, away, [], prepared, targets, sums, up, smoothing)
        up = ring_shift(up, 1)
        if away > 1:
            (down,) = ring_step(here, 1 - away, [], prepared, targets, sums, down, smoothing)
            down = ring_shift(down, -1)
    (own,) = ring_step(here, 0, [], prepared, targets, sums, None, smoothing)

    keep, give = pl.pallas_call(
        merge_kernel,
        out_shape=(jax.ShapeDtypeStruct((block, systems), jnp.float32),) * 2,
        in_specs=[SMEM] + [VMEM] * 3,
        out_specs=(VMEM, VMEM),
        compiler_params=small,
        name="merge",
    )(here, own, up, down)
    applied, shares = pl.pallas_call(
        functools.partial(products_kernel, 1.0 / math.sqrt(total)),
        out_shape=(
            jax.ShapeDtypeStruct((systems, block), jnp.float32),
            jax.ShapeDtypeStruct((lax.axis_size(PLANE), 1, 4 * systems), jnp.float32),
        ),
        in_specs=[VMEM] * 5,
        out_specs=(VMEM, VMEM),
        compiler_params=small,
        name="products",
    )(keep, shift(give, "c", 1), self_term[None, :], residual, direction)
    shares = pl.pallas_call(
        spread_kernel,
        out_shape=jax.ShapeDtypeStruct((ring, 1, 4 * systems), jnp.float32),
        in_specs=[VMEM],
        out_specs=VMEM,
        compiler_params=small,
        name="spread",
    )(lax.all_to_all(shares, PLANE, 0, 0))
    return pl.pallas_call(
        update_kernel,
        out_shape=(jax.ShapeDtypeStruct((systems, block), jnp.float32),) * 3,
        in_specs=[VMEM] * 5,
        out_specs=(VMEM,) * 3,
        compiler_params=small,
        name="update",
    )(lax.all_to_all(shares, RING, 0, 0), solution, residual, direction, applied)


def solution(mesh):
    fine = Mesh(mesh.devices.reshape(SIZES), FINE)
    matrix = P(None, FINE)
    return jax.shard_map(
        on_device,
        mesh=fine,
        in_specs=(matrix, P(FINE), matrix, matrix, matrix),
        out_specs=(matrix, matrix, matrix),
        check_vma=False,
    )
```

```python
import functools
import math

import jax
import jax.numpy as jnp
from jax import lax
from jax.experimental import pallas as pl
from jax.experimental.pallas import tpu as pltpu
from jax.sharding import Mesh, PartitionSpec as P

FINE = ("x", "zl", "c", "y", "zh")
SIZES = (4, 2, 2, 4, 4)
RING = ("zl", "zh")
TARGETS = ("zl", "c", "zh")
PLANE = ("x", "c", "y")
PART = 256
LANES = 256
COORDS = 8
VMEM = pl.BlockSpec(memory_space=pltpu.VMEM)
SMEM = pl.BlockSpec(memory_space=pltpu.SMEM)


def shift(value, axes, by):
    size = lax.axis_size(axes)
    return lax.ppermute(value, axes, [(i, (i + by) % size) for i in range(size)])


def ring_index(z):
    return (z % 2) * SIZES[4] + z // 2


def ring_shift(value, by):
    size = lax.axis_size(RING)
    return lax.ppermute(value, RING, [(ring_index(z), ring_index((z + by) % size)) for z in range(size)])


def pack_kernel(points, direction, mine, coords, held, sems):
    systems = direction.shape[0]
    first = pltpu.make_async_copy(points, held, sems.at[0])
    second = pltpu.make_async_copy(direction, mine.at[pl.ds(0, systems)], sems.at[1])
    first.start()
    second.start()
    first.wait()
    spread = jnp.concatenate([held[...], jnp.zeros((COORDS - 3, held.shape[1]), jnp.float32)], axis=0)
    mine[systems:, :] = spread
    coords[...] = jnp.broadcast_to(spread[None], coords.shape)
    second.wait()


def prepare(groups, weights, rows):
    systems = weights.shape[0] // 2
    at = 0
    for group in groups:
        for b in range(group.shape[0]):
            block = group.shape[2]
            cols = slice(at, at + block)
            values = group[b, :systems, :]
            high = values.astype(jnp.bfloat16)
            weights[:systems, cols] = high
            weights[systems:, cols] = (values - high.astype(jnp.float32)).astype(jnp.bfloat16)
            for i in range(3):
                rows[8 * i : 8 * i + 8, cols] = jnp.broadcast_to(group[b, systems + i : systems + i + 1, :], (8, block))
            at += block


def accumulate(smoothing, wide, weights, rows, columns, out, tile_a, tile_b):
    systems = out.shape[1]
    across = weights.shape[1] // wide
    parts = out.shape[0] // PART
    assert parts == 2 or across == 1
    pairs = parts * across // 2
    tiles = (tile_a, tile_b)

    def at(pair, half):
        if across == 1:
            return pl.ds(pl.multiple_of((2 * pair + half) * PART, PART), PART), pl.ds(0, wide)
        return pl.ds(half * PART, PART), pl.ds(pl.multiple_of(pair * wide, wide), wide)

    def make(place, tile):
        down, columns_here = place
        for r in range(0, PART, 16):
            here = [jnp.broadcast_to(columns[pl.ds(down.start + r, 16), i : i + 1], (16, LANES)) for i in range(3)]
            for c in range(0, wide, LANES):
                lanes = pl.ds(columns_here.start + c, LANES)
                far = [jnp.concatenate([rows[8 * i : 8 * i + 8, lanes]] * 2, axis=0) for i in range(3)]
                dx, dy, dz = (far[i] - here[i] for i in range(3))
                kernel = lax.rsqrt(dx * dx + dy * dy + (dz * dz + smoothing * smoothing))
                high = kernel.astype(jnp.bfloat16)
                low = (kernel - high.astype(jnp.float32)).astype(jnp.bfloat16)
                tile[r : r + 16, c : c + LANES] = high
                tile[PART + r : PART + r + 16, c : c + LANES] = low

    def multiply(place, tile):
        down, columns_here = place
        product = lax.dot_general(
            tile[...],
            weights[:, columns_here],
            (((1,), (1,)), ((), ())),
            preferred_element_type=jnp.float32,
        )
        out[down, :] += (product[:PART, :systems] + product[PART:, systems:]) + (
            product[:PART, systems:] + product[PART:, :systems]
        )

    make(at(0, 0), tile_a)

    def two_steps(pair, carry):
        make(at(pair, 1), tile_b)
        multiply(at(pair, 0), tile_a)
        make(at(jnp.minimum(pair + 1, pairs - 1), 0), tile_a)
        multiply(at(pair, 1), tile_b)
        return carry

    lax.fori_loop(0, pairs, two_steps, 0)


def bulk_kernel(smoothing, wide, count, started, *refs):
    groups, refs = refs[:count], refs[count:]
    target, refs = refs[0], refs[1:]
    before, refs = (refs[0], refs[1:]) if started else (None, refs)
    out, weights, rows, columns, tile_a, tile_b = refs
    block = target.shape[2]
    for b in range(target.shape[0]):
        columns[b * block : (b + 1) * block, :] = jnp.transpose(target[b])
    prepare(groups, weights, rows)
    out[...] = before[...] if started else jnp.zeros_like(out)
    accumulate(smoothing, wide, weights, rows, columns, out, tile_a, tile_b)


def step_kernel(smoothing, wide, offset, count, arrived, *refs):
    here, refs = refs[0], refs[1:]
    groups, refs = refs[:count], refs[count:]
    if not count:
        weights, rows, refs = refs[0], refs[1], refs[2:]
    target, before, refs = refs[0], refs[1], refs[2:]
    came, refs = (refs[0], refs[1:]) if arrived else (None, refs)
    out, refs = refs[0], refs[1:]
    if count:
        weights, rows, refs = refs[0], refs[1], refs[2:]
        prepare(groups, weights, rows)
    columns, tile_a, tile_b = refs
    chips = target.shape[0] // 2
    z = lax.rem(here[0] + offset, chips)
    block = target.shape[2]
    for core in range(2):
        which = lax.rem(z, 2) * chips + core * (chips // 2) + lax.div(z, 2)
        rows_of_core = slice(core * block, (core + 1) * block)
        columns[rows_of_core, :] = jnp.transpose(target[which])
        earlier = before[pl.ds(pl.multiple_of(which * block, block), block), :]
        out[rows_of_core, :] = earlier + came[rows_of_core, :] if arrived else earlier
    accumulate(smoothing, wide, weights, rows, columns, out, tile_a, tile_b)


def cost(targets, sources, systems):
    return pl.CostEstimate(
        flops=16 * targets * sources * systems, bytes_accessed=4 * targets * systems, transcendentals=targets * sources
    )


def bulk(groups, targets, before, smoothing, wide=1792):
    ring, coords, block = targets.shape
    systems = groups[0].shape[1] - coords
    sources = sum(g.shape[0] for g in groups) * block
    started = before is not None
    return pl.pallas_call(
        functools.partial(bulk_kernel, smoothing, wide, len(groups), started),
        out_shape=jax.ShapeDtypeStruct((ring * block, systems), jnp.float32),
        in_specs=[VMEM] * (len(groups) + 1 + started),
        out_specs=VMEM,
        scratch_shapes=[
            pltpu.VMEM((2 * systems, sources), jnp.bfloat16),
            pltpu.VMEM((24, sources), jnp.float32),
            pltpu.VMEM((ring * block, coords), jnp.float32),
            pltpu.VMEM((2 * PART, wide), jnp.bfloat16),
            pltpu.VMEM((2 * PART, wide), jnp.bfloat16),
        ],
        compiler_params=pltpu.CompilerParams(vmem_limit_bytes=24 * 2**20),
        cost_estimate=cost(ring * block, sources, systems),
        name="bulk",
    )(*groups, targets, *([before] if started else []))


def ring_step(here, offset, groups, prepared, targets, before, arrived, smoothing, wide=768):
    shards, coords, block = targets.shape
    systems = before.shape[1]
    sources = prepared[0].shape[1] if prepared else sum(g.shape[0] for g in groups) * block
    came = [] if arrived is None else [arrived]
    outs = [jax.ShapeDtypeStruct((2 * block, systems), jnp.float32)]
    if groups:
        outs += [
            jax.ShapeDtypeStruct((2 * systems, sources), jnp.bfloat16),
            jax.ShapeDtypeStruct((24, sources), jnp.float32),
        ]
    operands = [*groups, *prepared, targets, before, *came]
    return pl.pallas_call(
        functools.partial(step_kernel, smoothing, wide, offset % (shards // 2), len(groups), bool(came)),
        out_shape=outs,
        in_specs=[SMEM] + [VMEM] * len(operands),
        out_specs=[VMEM] * len(outs),
        scratch_shapes=[
            pltpu.VMEM((2 * block, coords), jnp.float32),
            pltpu.VMEM((2 * PART, wide), jnp.bfloat16),
            pltpu.VMEM((2 * PART, wide), jnp.bfloat16),
        ],
        compiler_params=pltpu.CompilerParams(vmem_limit_bytes=24 * 2**20),
        cost_estimate=cost(2 * block, sources, systems),
        name="ring_step",
    )(here, *operands)


def column_sums(values):
    half = values.shape[1] // 2
    return jnp.sum(jnp.transpose(values[:, :half] + values[:, half:]), axis=0, keepdims=True)


def merge_kernel(here, own, up, down, keep, give):
    block = keep.shape[0]
    for out, core in ((keep, here[1]), (give, 1 - here[1])):
        at = pl.ds(pl.multiple_of(core * block, block), block)
        out[...] = (own[at, :] + up[at, :]) + down[at, :]


def products_kernel(scale, kept, got, self_term, residual_ref, direction_ref, applied_ref, sums_ref):
    total = kept[...] + got[...]
    direction = direction_ref[...]
    residual = residual_ref[...]
    applied = self_term[...] * direction + jnp.transpose(total) * scale
    applied_ref[...] = applied
    sums = jnp.concatenate(
        [
            column_sums(residual * residual),
            column_sums(direction * applied),
            column_sums(residual * applied),
            column_sums(applied * applied),
        ],
        axis=1,
    )
    sums_ref[...] = jnp.broadcast_to(sums[None], sums_ref.shape)


def spread_kernel(parts, out):
    out[...] = jnp.broadcast_to(jnp.sum(parts[...], axis=0, keepdims=True), out.shape)


def update_kernel(
    sums_ref, solution_ref, residual_ref, direction_ref, applied_ref, solution_out, residual_out, direction_out
):
    systems = solution_ref.shape[0]
    sums = jnp.sum(sums_ref[...], axis=0)
    norm_now, curvature, cross, image = (sums[:, i * systems : (i + 1) * systems] for i in range(4))
    step_len = norm_now / (curvature + 1e-06)
    norm_next = jnp.maximum(norm_now + step_len * (step_len * image - 2.0 * cross), 0.0)
    factor = norm_next / (norm_now + 1e-06)
    step_len = jnp.transpose(jnp.broadcast_to(step_len, (systems, systems)))
    factor = jnp.transpose(jnp.broadcast_to(factor, (systems, systems)))
    for c in range(0, solution_ref.shape[1], systems):
        cols = slice(c, c + systems)
        direction = direction_ref[:, cols]
        residual_next = residual_ref[:, cols] - step_len * applied_ref[:, cols]
        solution_out[:, cols] = solution_ref[:, cols] + step_len * direction
        residual_out[:, cols] = residual_next
        direction_out[:, cols] = residual_next + factor * direction


def on_device(points, self_term, solution, residual, direction):
    systems, block = direction.shape
    total = block * math.prod(SIZES)
    smoothing = 1.0 / math.sqrt(total)
    ring = lax.axis_size(RING)
    here = jnp.stack([lax.axis_index("zh") * 2 + lax.axis_index("zl"), lax.axis_index("c")])
    small = pltpu.CompilerParams(vmem_limit_bytes=16 * 2**20)

    mine, coords = pl.pallas_call(
        pack_kernel,
        out_shape=(
            jax.ShapeDtypeStruct((systems + COORDS, block), jnp.float32),
            jax.ShapeDtypeStruct((2 * ring, COORDS, block), jnp.float32),
        ),
        in_specs=[pl.BlockSpec(memory_space=pl.ANY)] * 2,
        out_specs=(VMEM, VMEM),
        scratch_shapes=[pltpu.VMEM(points.shape, jnp.float32), pltpu.SemaphoreType.DMA((2,))],
        compiler_params=small,
        name="pack",
    )(points, direction)
    line = [shift(mine, "x", by) for by in (1, -1, 2)]
    column = [shift(mine, "y", by) for by in (1, -1, 2)]
    line[0], coords = lax.optimization_barrier((line[0], coords))
    targets = lax.all_to_all(coords, TARGETS, 0, 0)
    targets, *line = lax.optimization_barrier((targets, *line))
    line = jnp.stack(line)
    rest = [shift(line, "y", 1), shift(line, "y", -1)] + [shift(column[2][None], "x", by) for by in (1, -1, 2)]
    sums = bulk([mine[None], line] + [part[None] for part in column], targets, None, smoothing)
    sums, *rest = lax.optimization_barrier((sums, *rest))

    up, *prepared = ring_step(here, 4, rest, [], targets, sums, None, smoothing)
    up = ring_shift(up, 1)
    (down,) = ring_step(here, -3, [], prepared, targets, sums, None, smoothing)
    down = ring_shift(down, -1)
    for away in (3, 2, 1):
        (up,) = ring_step(here, away, [], prepared, targets, sums, up, smoothing)
        up = ring_shift(up, 1)
        if away > 1:
            (down,) = ring_step(here, 1 - away, [], prepared, targets, sums, down, smoothing)
            down = ring_shift(down, -1)
    (own,) = ring_step(here, 0, [], prepared, targets, sums, None, smoothing)

    keep, give = pl.pallas_call(
        merge_kernel,
        out_shape=(jax.ShapeDtypeStruct((block, systems), jnp.float32),) * 2,
        in_specs=[SMEM] + [VMEM] * 3,
        out_specs=(VMEM, VMEM),
        compiler_params=small,
        name="merge",
    )(here, own, up, down)
    applied, shares = pl.pallas_call(
        functools.partial(products_kernel, 1.0 / math.sqrt(total)),
        out_shape=(
            jax.ShapeDtypeStruct((systems, block), jnp.float32),
            jax.ShapeDtypeStruct((lax.axis_size(PLANE), 1, 4 * systems), jnp.float32),
        ),
        in_specs=[VMEM] * 5,
        out_specs=(VMEM, VMEM),
        compiler_params=small,
        name="products",
    )(keep, shift(give, "c", 1), self_term[None, :], residual, direction)
    shares = pl.pallas_call(
        spread_kernel,
        out_shape=jax.ShapeDtypeStruct((ring, 1, 4 * systems), jnp.float32),
        in_specs=[VMEM],
        out_specs=VMEM,
        compiler_params=small,
        name="spread",
    )(lax.all_to_all(shares, PLANE, 0, 0))
    return pl.pallas_call(
        update_kernel,
        out_shape=(jax.ShapeDtypeStruct((systems, block), jnp.float32),) * 3,
        in_specs=[VMEM] * 5,
        out_specs=(VMEM,) * 3,
        compiler_params=small,
        name="update",
    )(lax.all_to_all(shares, RING, 0, 0), solution, residual, direction, applied)


def solution(mesh):
    fine = Mesh(mesh.devices.reshape(SIZES), FINE)
    matrix = P(None, FINE)
    return jax.shard_map(
        on_device,
        mesh=fine,
        in_specs=(matrix, P(FINE), matrix, matrix, matrix),
        out_specs=(matrix, matrix, matrix),
        check_vma=False,
    )
```

```python
import functools
import math

import jax
import jax.numpy as jnp
from jax import lax
from jax.experimental import pallas as pl
from jax.experimental.pallas import tpu as pltpu
from jax.sharding import Mesh, PartitionSpec as P

FINE = ("x", "zl", "c", "y", "zh")
SIZES = (4, 2, 2, 4, 4)
RING = ("zl", "zh")
PLANE = ("x", "c", "y")
PART = 256
LANES = 256
COORDS = 8
KERNEL_VMEM = 10 * 2**20
VMEM = pl.BlockSpec(memory_space=pltpu.VMEM)
SMEM = pl.BlockSpec(memory_space=pltpu.SMEM)


def shift(value, axes, by):
    size = lax.axis_size(axes)
    return lax.ppermute(value, axes, [(i, (i + by) % size) for i in range(size)])


def ring_index(z):
    return (z % 2) * SIZES[4] + z // 2


def ring_shift(value, by):
    size = lax.axis_size(RING)
    return lax.ppermute(value, RING, [(ring_index(z), ring_index((z + by) % size)) for z in range(size)])


def pack_kernel(points, direction, mine, coords):
    systems = direction.shape[0]
    mine[...] = jnp.zeros_like(mine)
    mine[:systems, :] = direction[...]
    mine[systems : systems + 3, :] = points[...]
    coords[...] = jnp.broadcast_to(mine[systems:, :][None], coords.shape)


def prepare(groups, weights, rows):
    systems = weights.shape[0] // 2
    at = 0
    for group in groups:
        for b in range(group.shape[0]):
            block = group.shape[2]
            cols = slice(at, at + block)
            values = group[b, :systems, :]
            high = values.astype(jnp.bfloat16)
            weights[:systems, cols] = high
            weights[systems:, cols] = (values - high.astype(jnp.float32)).astype(jnp.bfloat16)
            for i in range(3):
                rows[8 * i : 8 * i + 8, cols] = jnp.broadcast_to(group[b, systems + i : systems + i + 1, :], (8, block))
            at += block


def accumulate(smoothing, wide, pairs, at, weights, rows, columns, out, tile_a, tile_b):
    systems = out.shape[1]

    def make(place, tile):
        first, column = place
        for r in range(0, PART, 16):
            here = [jnp.broadcast_to(columns[pl.ds(first + r, 16), i : i + 1], (16, LANES)) for i in range(3)]
            for c in range(0, wide, LANES):
                lanes = pl.ds(column + c, LANES)
                far = [jnp.concatenate([rows[8 * i : 8 * i + 8, lanes]] * 2, axis=0) for i in range(3)]
                dx, dy, dz = (far[i] - here[i] for i in range(3))
                kernel = lax.rsqrt(dx * dx + dy * dy + (dz * dz + smoothing * smoothing))
                high = kernel.astype(jnp.bfloat16)
                low = (kernel - high.astype(jnp.float32)).astype(jnp.bfloat16)
                tile[r : r + 16, c : c + LANES] = high
                tile[PART + r : PART + r + 16, c : c + LANES] = low

    def multiply(place, tile):
        first, column = place
        product = lax.dot_general(
            tile[...],
            weights[:, pl.ds(column, wide)],
            (((1,), (1,)), ((), ())),
            preferred_element_type=jnp.float32,
        )
        out[pl.ds(first, PART), :] += (product[:PART, :systems] + product[PART:, systems:]) + (
            product[:PART, systems:] + product[PART:, :systems]
        )

    make(at(0, 0), tile_a)

    def two_steps(pair, carry):
        make(at(pair, 1), tile_b)
        multiply(at(pair, 0), tile_a)
        make(at(jnp.minimum(pair + 1, pairs - 1), 0), tile_a)
        multiply(at(pair, 1), tile_b)
        return carry

    lax.fori_loop(0, pairs, two_steps, 0)


def shard_at(z, offset, chips):
    z = lax.rem(z + offset, chips)
    return lax.rem(z, 2) * (chips // 2) + lax.div(z, 2)


def bulk_kernel(smoothing, wide, count, started, here, *refs):
    groups, refs = refs[:count], refs[count:]
    target, refs = refs[0], refs[1:]
    before, refs = (refs[0], refs[1:]) if started else (None, refs)
    out, weights, rows, columns, tile_a, tile_b = refs
    chips, _, block = target.shape
    for b in range(chips):
        columns[b * block : (b + 1) * block, :] = jnp.transpose(target[b])
    prepare(groups, weights, rows)
    out[...] = before[...] if started else jnp.zeros_like(out)

    def at(pair, half):
        shard = shard_at(here[0], pair + 1, chips) if started else pair
        return pl.multiple_of(shard * block, block), half * wide

    accumulate(smoothing, wide, chips - started, at, weights, rows, columns, out, tile_a, tile_b)


def step_kernel(smoothing, wide, offset, count, sets, arrived, here, *refs):
    groups, refs = refs[:count], refs[count:]
    prepared, refs = refs[: 2 * sets], refs[2 * sets :]
    target, before, refs = refs[0], refs[1], refs[2:]
    came, refs = (refs[0], refs[1:]) if arrived else (None, refs)
    out, refs = refs[0], refs[1:]
    if count:
        prepared, refs = refs[:2], refs[2:]
        prepare(groups, *prepared)
    columns, tile_a, tile_b = refs
    chips, _, block = target.shape
    which = shard_at(here[0], offset, chips)
    columns[...] = jnp.transpose(target[which])
    earlier = before[pl.ds(pl.multiple_of(which * block, block), block), :]
    out[...] = earlier + came[...] if arrived else earlier

    def at(pair, half):
        return 0, pl.multiple_of((2 * pair + half) * wide, wide)

    for i in range(0, len(prepared), 2):
        weights, rows = prepared[i : i + 2]
        pairs = weights.shape[1] // (2 * wide)
        accumulate(smoothing, wide, pairs, at, weights, rows, columns, out, tile_a, tile_b)


def cost(targets, sources, systems):
    return pl.CostEstimate(
        flops=16 * targets * sources * systems, bytes_accessed=4 * targets * systems, transcendentals=targets * sources
    )


def prepared_shapes(systems, sources):
    return [
        jax.ShapeDtypeStruct((2 * systems, sources), jnp.bfloat16),
        jax.ShapeDtypeStruct((24, sources), jnp.float32),
    ]


def bulk(here, groups, targets, before, smoothing):
    chips, coords, block = targets.shape
    systems = groups[0].shape[1] - coords
    sources = sum(g.shape[0] for g in groups) * block
    wide = sources // 2
    started = before is not None
    held = prepared_shapes(systems, sources)
    return pl.pallas_call(
        functools.partial(bulk_kernel, smoothing, wide, len(groups), started),
        out_shape=[jax.ShapeDtypeStruct((chips * block, systems), jnp.float32)] + (held if started else []),
        in_specs=[SMEM] + [VMEM] * (len(groups) + 1 + started),
        out_specs=[VMEM] * (3 if started else 1),
        scratch_shapes=([] if started else [pltpu.VMEM(h.shape, h.dtype) for h in held])
        + [
            pltpu.VMEM((chips * block, coords), jnp.float32),
            pltpu.VMEM((2 * PART, wide), jnp.bfloat16),
            pltpu.VMEM((2 * PART, wide), jnp.bfloat16),
        ],
        compiler_params=pltpu.CompilerParams(vmem_limit_bytes=KERNEL_VMEM),
        cost_estimate=cost(chips * block, sources, systems),
        name="bulk",
    )(here, *groups, targets, *([before] if started else []))


def ring_step(here, offset, groups, prepared, targets, before, arrived, smoothing, wide=512):
    chips, coords, block = targets.shape
    systems = before.shape[1]
    sources = sum(g.shape[0] for g in groups) * block + sum(p.shape[1] for p in prepared[::2])
    came = [] if arrived is None else [arrived]
    outs = [jax.ShapeDtypeStruct((block, systems), jnp.float32)]
    if groups:
        outs += prepared_shapes(systems, sources)
    operands = [*groups, *prepared, targets, before, *came]
    return pl.pallas_call(
        functools.partial(step_kernel, smoothing, wide, offset % chips, len(groups), len(prepared) // 2, bool(came)),
        out_shape=outs,
        in_specs=[SMEM] + [VMEM] * len(operands),
        out_specs=[VMEM] * len(outs),
        scratch_shapes=[
            pltpu.VMEM((block, coords), jnp.float32),
            pltpu.VMEM((2 * PART, wide), jnp.bfloat16),
            pltpu.VMEM((2 * PART, wide), jnp.bfloat16),
        ],
        compiler_params=pltpu.CompilerParams(vmem_limit_bytes=KERNEL_VMEM),
        cost_estimate=cost(block, sources, systems),
        name="ring_step",
    )(here, *operands)


def column_sums(values):
    half = values.shape[1] // 2
    return jnp.sum(jnp.transpose(values[:, :half] + values[:, half:]), axis=0, keepdims=True)


def products_kernel(scale, own, up, down, self_term, residual_ref, direction_ref, applied_ref, sums_ref):
    total = (own[...] + up[...]) + down[...]
    direction = direction_ref[...]
    residual = residual_ref[...]
    applied = self_term[...] * direction + jnp.transpose(total) * scale
    applied_ref[...] = applied
    sums = jnp.concatenate(
        [
            column_sums(residual * residual),
            column_sums(direction * applied),
            column_sums(residual * applied),
            column_sums(applied * applied),
        ],
        axis=1,
    )
    sums_ref[...] = jnp.broadcast_to(sums[None], sums_ref.shape)


def spread_kernel(parts, out):
    out[...] = jnp.broadcast_to(jnp.sum(parts[...], axis=0, keepdims=True), out.shape)


def update_kernel(
    sums_ref, solution_ref, residual_ref, direction_ref, applied_ref, solution_out, residual_out, direction_out
):
    systems = solution_ref.shape[0]
    sums = jnp.sum(sums_ref[...], axis=0)
    norm_now, curvature, cross, image = (sums[:, i * systems : (i + 1) * systems] for i in range(4))
    step_len = norm_now / (curvature + 1e-06)
    norm_next = jnp.maximum(norm_now + step_len * (step_len * image - 2.0 * cross), 0.0)
    factor = norm_next / (norm_now + 1e-06)
    step_len = jnp.transpose(jnp.broadcast_to(step_len, (systems, systems)))
    factor = jnp.transpose(jnp.broadcast_to(factor, (systems, systems)))
    for c in range(0, solution_ref.shape[1], systems):
        cols = slice(c, c + systems)
        direction = direction_ref[:, cols]
        residual_next = residual_ref[:, cols] - step_len * applied_ref[:, cols]
        solution_out[:, cols] = solution_ref[:, cols] + step_len * direction
        residual_out[:, cols] = residual_next
        direction_out[:, cols] = residual_next + factor * direction


def on_device(points, self_term, solution, residual, direction):
    systems, block = direction.shape
    total = block * math.prod(SIZES)
    smoothing = 1.0 / math.sqrt(total)
    ring = lax.axis_size(RING)
    here = jnp.reshape(lax.axis_index("zh") * 2 + lax.axis_index("zl"), (1,))
    small = pltpu.CompilerParams(vmem_limit_bytes=16 * 2**20)

    mine, coords = pl.pallas_call(
        pack_kernel,
        out_shape=(
            jax.ShapeDtypeStruct((systems + COORDS, block), jnp.float32),
            jax.ShapeDtypeStruct((ring, COORDS, block), jnp.float32),
        ),
        in_specs=[VMEM] * 2,
        out_specs=(VMEM, VMEM),
        compiler_params=small,
        name="pack",
    )(points, direction)
    near = [shift(mine, "x", 1), shift(mine, "x", -1), shift(mine, "x", 2)]
    coords, *near = lax.optimization_barrier((coords, *near))
    targets = lax.all_to_all(coords, RING, 0, 0)
    line = jnp.stack([mine, *near])
    above, below = shift(line, "y", 1), shift(line, "y", -1)
    (sums,) = bulk(here, [line, shift(line, "c", 1)], targets, None, smoothing)
    sums, above, below = lax.optimization_barrier((sums, above, below))
    far = [shift(above[:2], "y", 1), shift(below[2:], "y", -1)]
    copies = [shift(above, "c", 1), shift(below, "c", 1)]
    sums, *second = bulk(here, [above, below], targets, sums, smoothing)
    sums, *far = lax.optimization_barrier((sums, *far))
    last = copies + far + [shift(part, "c", 1) for part in far]

    up, *third = ring_step(here, 4, last, [], targets, sums, None, smoothing)
    up = ring_shift(up, 1)
    (down,) = ring_step(here, -3, [], third, targets, sums, None, smoothing)
    down = ring_shift(down, -1)
    for away in (3, 2, 1):
        (up,) = ring_step(here, away, [], third, targets, sums, up, smoothing)
        up = ring_shift(up, 1)
        if away > 1:
            (down,) = ring_step(here, 1 - away, [], third, targets, sums, down, smoothing)
            down = ring_shift(down, -1)
    (own,) = ring_step(here, 0, [], second + third, targets, sums, None, smoothing)

    applied, shares = pl.pallas_call(
        functools.partial(products_kernel, 1.0 / math.sqrt(total)),
        out_shape=(
            jax.ShapeDtypeStruct((systems, block), jnp.float32),
            jax.ShapeDtypeStruct((lax.axis_size(PLANE), 1, 4 * systems), jnp.float32),
        ),
        in_specs=[VMEM] * 6,
        out_specs=(VMEM, VMEM),
        compiler_params=small,
        name="products",
    )(own, up, down, self_term[None, :], residual, direction)
    shares = pl.pallas_call(
        spread_kernel,
        out_shape=jax.ShapeDtypeStruct((ring, 1, 4 * systems), jnp.float32),
        in_specs=[VMEM],
        out_specs=VMEM,
        compiler_params=small,
        name="spread",
    )(lax.all_to_all(shares, PLANE, 0, 0))
    return pl.pallas_call(
        update_kernel,
        out_shape=(jax.ShapeDtypeStruct((systems, block), jnp.float32),) * 3,
        in_specs=[VMEM] * 5,
        out_specs=(VMEM,) * 3,
        compiler_params=small,
        name="update",
    )(lax.all_to_all(shares, RING, 0, 0), solution, residual, direction, applied)


def solution(mesh):
    fine = Mesh(mesh.devices.reshape(SIZES), FINE)
    matrix = P(None, FINE)
    return jax.shard_map(
        on_device,
        mesh=fine,
        in_specs=(matrix, P(FINE), matrix, matrix, matrix),
        out_specs=(matrix, matrix, matrix),
        check_vma=False,
    )
```

```python
import functools
import math

import jax
import jax.numpy as jnp
from jax import lax
from jax.experimental import pallas as pl
from jax.experimental.pallas import tpu as pltpu
from jax.sharding import Mesh, PartitionSpec as P

FINE = ("x", "zl", "c", "y", "zh")
SIZES = (4, 2, 2, 4, 4)
RING = ("zl", "zh")
PLANE = ("x", "c", "y")
PART = 256
LANES = 1024
COORDS = 8
KERNEL_VMEM = 10 * 2**20
VMEM = pl.BlockSpec(memory_space=pltpu.VMEM)
SMEM = pl.BlockSpec(memory_space=pltpu.SMEM)


def shift(value, axes, by):
    size = lax.axis_size(axes)
    return lax.ppermute(value, axes, [(i, (i + by) % size) for i in range(size)])


def ring_index(z):
    return (z % 2) * SIZES[4] + z // 2


def ring_shift(value, by):
    size = lax.axis_size(RING)
    return lax.ppermute(value, RING, [(ring_index(z), ring_index((z + by) % size)) for z in range(size)])


def pack_kernel(points, direction, mine, coords):
    systems = direction.shape[0]
    mine[...] = jnp.zeros_like(mine)
    mine[:systems, :] = direction[...]
    mine[systems : systems + 3, :] = points[...]
    coords[...] = jnp.broadcast_to(mine[systems:, :][None], coords.shape)


def prepare(groups, weights, rows):
    systems = weights.shape[0] // 2
    at = 0
    for group in groups:
        for b in range(group.shape[0]):
            block = group.shape[2]
            cols = slice(at, at + block)
            values = group[b, :systems, :]
            high = values.astype(jnp.bfloat16)
            weights[:systems, cols] = high
            weights[systems:, cols] = (values - high.astype(jnp.float32)).astype(jnp.bfloat16)
            for i in range(3):
                rows[8 * i : 8 * i + 8, cols] = jnp.broadcast_to(group[b, systems + i : systems + i + 1, :], (8, block))
            at += block


def accumulate(smoothing, wide, pairs, at, weights, rows, columns, out, tile_a, tile_b):
    systems = out.shape[1]

    def make(place, tile):
        first, column = place
        step = min(wide, LANES)
        for r in range(0, PART, 16):
            here = [jnp.broadcast_to(columns[pl.ds(first + r, 16), i : i + 1], (16, step)) for i in range(3)]
            for c in range(0, wide, step):
                lanes = pl.ds(column + c, step)
                far = [jnp.concatenate([rows[8 * i : 8 * i + 8, lanes]] * 2, axis=0) for i in range(3)]
                dx, dy, dz = (far[i] - here[i] for i in range(3))
                kernel = lax.rsqrt(dx * dx + dy * dy + (dz * dz + smoothing * smoothing))
                high = kernel.astype(jnp.bfloat16)
                low = (kernel - high.astype(jnp.float32)).astype(jnp.bfloat16)
                tile[r : r + 16, c : c + step] = high
                tile[PART + r : PART + r + 16, c : c + step] = low

    def multiply(place, tile):
        first, column = place
        product = lax.dot_general(
            tile[...],
            weights[:, pl.ds(column, wide)],
            (((1,), (1,)), ((), ())),
            preferred_element_type=jnp.float32,
        )
        out[pl.ds(first, PART), :] += (product[:PART, :systems] + product[PART:, systems:]) + (
            product[:PART, systems:] + product[PART:, :systems]
        )

    make(at(0, 0), tile_a)

    def two_steps(pair, carry):
        make(at(pair, 1), tile_b)
        multiply(at(pair, 0), tile_a)
        make(at(jnp.minimum(pair + 1, pairs - 1), 0), tile_a)
        multiply(at(pair, 1), tile_b)
        return carry

    lax.fori_loop(0, pairs, two_steps, 0)


def shard_at(z, offset, chips):
    z = lax.rem(z + offset, chips)
    return lax.rem(z, 2) * (chips // 2) + lax.div(z, 2)


def bulk_kernel(smoothing, wide, count, started, here, *refs):
    groups, refs = refs[:count], refs[count:]
    target, refs = refs[0], refs[1:]
    before, refs = (refs[0], refs[1:]) if started else (None, refs)
    out, weights, rows, columns, tile_a, tile_b = refs
    chips, _, block = target.shape
    for b in range(chips):
        columns[b * block : (b + 1) * block, :] = jnp.transpose(target[b])
    prepare(groups, weights, rows)
    out[...] = before[...] if started else jnp.zeros_like(out)

    def at(pair, half):
        shard = shard_at(here[0], pair + 1, chips) if started else pair
        return pl.multiple_of(shard * block, block), half * wide

    accumulate(smoothing, wide, chips - started, at, weights, rows, columns, out, tile_a, tile_b)


def step_kernel(smoothing, wide, offset, count, sets, arrived, here, *refs):
    groups, refs = refs[:count], refs[count:]
    prepared, refs = refs[: 2 * sets], refs[2 * sets :]
    target, before, refs = refs[0], refs[1], refs[2:]
    came, refs = (refs[0], refs[1:]) if arrived else (None, refs)
    out, refs = refs[0], refs[1:]
    if count:
        prepared, refs = refs[:2], refs[2:]
        prepare(groups, *prepared)
    columns, tile_a, tile_b = refs
    chips, _, block = target.shape
    which = shard_at(here[0], offset, chips)
    columns[...] = jnp.transpose(target[which])
    earlier = before[pl.ds(pl.multiple_of(which * block, block), block), :]
    out[...] = earlier + came[...] if arrived else earlier

    def at(pair, half):
        return 0, pl.multiple_of((2 * pair + half) * wide, wide)

    for i in range(0, len(prepared), 2):
        weights, rows = prepared[i : i + 2]
        pairs = weights.shape[1] // (2 * wide)
        accumulate(smoothing, wide, pairs, at, weights, rows, columns, out, tile_a, tile_b)


def cost(targets, sources, systems):
    return pl.CostEstimate(
        flops=16 * targets * sources * systems, bytes_accessed=4 * targets * systems, transcendentals=targets * sources
    )


def prepared_shapes(systems, sources):
    return [
        jax.ShapeDtypeStruct((2 * systems, sources), jnp.bfloat16),
        jax.ShapeDtypeStruct((24, sources), jnp.float32),
    ]


def bulk(here, groups, targets, before, smoothing):
    chips, coords, block = targets.shape
    systems = groups[0].shape[1] - coords
    sources = sum(g.shape[0] for g in groups) * block
    wide = sources // 2
    started = before is not None
    held = prepared_shapes(systems, sources)
    return pl.pallas_call(
        functools.partial(bulk_kernel, smoothing, wide, len(groups), started),
        out_shape=[jax.ShapeDtypeStruct((chips * block, systems), jnp.float32)] + (held if started else []),
        in_specs=[SMEM] + [VMEM] * (len(groups) + 1 + started),
        out_specs=[VMEM] * (3 if started else 1),
        scratch_shapes=([] if started else [pltpu.VMEM(h.shape, h.dtype) for h in held])
        + [
            pltpu.VMEM((chips * block, coords), jnp.float32),
            pltpu.VMEM((2 * PART, wide), jnp.bfloat16),
            pltpu.VMEM((2 * PART, wide), jnp.bfloat16),
        ],
        compiler_params=pltpu.CompilerParams(vmem_limit_bytes=KERNEL_VMEM),
        cost_estimate=cost(chips * block, sources, systems),
        name="bulk",
    )(here, *groups, targets, *([before] if started else []))


def ring_step(here, offset, groups, prepared, targets, before, arrived, smoothing, wide=512):
    chips, coords, block = targets.shape
    systems = before.shape[1]
    sources = sum(g.shape[0] for g in groups) * block + sum(p.shape[1] for p in prepared[::2])
    came = [] if arrived is None else [arrived]
    outs = [jax.ShapeDtypeStruct((block, systems), jnp.float32)]
    if groups:
        outs += prepared_shapes(systems, sources)
    operands = [*groups, *prepared, targets, before, *came]
    return pl.pallas_call(
        functools.partial(step_kernel, smoothing, wide, offset % chips, len(groups), len(prepared) // 2, bool(came)),
        out_shape=outs,
        in_specs=[SMEM] + [VMEM] * len(operands),
        out_specs=[VMEM] * len(outs),
        scratch_shapes=[
            pltpu.VMEM((block, coords), jnp.float32),
            pltpu.VMEM((2 * PART, wide), jnp.bfloat16),
            pltpu.VMEM((2 * PART, wide), jnp.bfloat16),
        ],
        compiler_params=pltpu.CompilerParams(vmem_limit_bytes=KERNEL_VMEM),
        cost_estimate=cost(block, sources, systems),
        name="ring_step",
    )(here, *operands)


def column_sums(values):
    half = values.shape[1] // 2
    return jnp.sum(jnp.transpose(values[:, :half] + values[:, half:]), axis=0, keepdims=True)


def products_kernel(scale, own, up, down, self_term, residual_ref, direction_ref, applied_ref, sums_ref):
    total = (own[...] + up[...]) + down[...]
    direction = direction_ref[...]
    residual = residual_ref[...]
    applied = self_term[...] * direction + jnp.transpose(total) * scale
    applied_ref[...] = applied
    sums = jnp.concatenate(
        [
            column_sums(residual * residual),
            column_sums(direction * applied),
            column_sums(residual * applied),
            column_sums(applied * applied),
        ],
        axis=1,
    )
    sums_ref[...] = jnp.broadcast_to(sums[None], sums_ref.shape)


def spread_kernel(parts, out):
    out[...] = jnp.broadcast_to(jnp.sum(parts[...], axis=0, keepdims=True), out.shape)


def update_kernel(
    sums_ref, solution_ref, residual_ref, direction_ref, applied_ref, solution_out, residual_out, direction_out
):
    systems = solution_ref.shape[0]
    sums = jnp.sum(sums_ref[...], axis=0)
    norm_now, curvature, cross, image = (sums[:, i * systems : (i + 1) * systems] for i in range(4))
    step_len = norm_now / (curvature + 1e-06)
    norm_next = jnp.maximum(norm_now + step_len * (step_len * image - 2.0 * cross), 0.0)
    factor = norm_next / (norm_now + 1e-06)
    step_len = jnp.transpose(jnp.broadcast_to(step_len, (systems, systems)))
    factor = jnp.transpose(jnp.broadcast_to(factor, (systems, systems)))
    for c in range(0, solution_ref.shape[1], systems):
        cols = slice(c, c + systems)
        direction = direction_ref[:, cols]
        residual_next = residual_ref[:, cols] - step_len * applied_ref[:, cols]
        solution_out[:, cols] = solution_ref[:, cols] + step_len * direction
        residual_out[:, cols] = residual_next
        direction_out[:, cols] = residual_next + factor * direction


def on_device(points, self_term, solution, residual, direction):
    systems, block = direction.shape
    total = block * math.prod(SIZES)
    smoothing = 1.0 / math.sqrt(total)
    ring = lax.axis_size(RING)
    here = jnp.reshape(lax.axis_index("zh") * 2 + lax.axis_index("zl"), (1,))
    small = pltpu.CompilerParams(vmem_limit_bytes=16 * 2**20)

    mine, coords = pl.pallas_call(
        pack_kernel,
        out_shape=(
            jax.ShapeDtypeStruct((systems + COORDS, block), jnp.float32),
            jax.ShapeDtypeStruct((ring, COORDS, block), jnp.float32),
        ),
        in_specs=[VMEM] * 2,
        out_specs=(VMEM, VMEM),
        compiler_params=small,
        name="pack",
    )(points, direction)
    targets = lax.all_to_all(coords, RING, 0, 0)
    near = [shift(mine, "x", 1), shift(mine, "x", -1), shift(mine, "x", 2)]
    targets, *near[1:] = lax.optimization_barrier((targets, *near[1:]))
    line = jnp.stack([mine, *near])
    above, below = shift(line, "y", 1), shift(line, "y", -1)
    (sums,) = bulk(here, [line, shift(line, "c", 1)], targets, None, smoothing)
    sums, above, below = lax.optimization_barrier((sums, above, below))
    far = [shift(above[:2], "y", 1), shift(below[2:], "y", -1)]
    copies = [shift(above, "c", 1), shift(below, "c", 1)]
    sums, *second = bulk(here, [above, below], targets, sums, smoothing)
    sums, *far = lax.optimization_barrier((sums, *far))
    last = copies + far + [shift(part, "c", 1) for part in far]

    up, *third = ring_step(here, 4, last, [], targets, sums, None, smoothing)
    up = ring_shift(up, 1)
    (down,) = ring_step(here, -3, [], third, targets, sums, None, smoothing)
    down = ring_shift(down, -1)
    for away in (3, 2, 1):
        (up,) = ring_step(here, away, [], third, targets, sums, up, smoothing)
        up = ring_shift(up, 1)
        if away > 1:
            (down,) = ring_step(here, 1 - away, [], third, targets, sums, down, smoothing)
            down = ring_shift(down, -1)
    (own,) = ring_step(here, 0, [], second + third, targets, sums, None, smoothing)

    applied, shares = pl.pallas_call(
        functools.partial(products_kernel, 1.0 / math.sqrt(total)),
        out_shape=(
            jax.ShapeDtypeStruct((systems, block), jnp.float32),
            jax.ShapeDtypeStruct((lax.axis_size(PLANE), 1, 4 * systems), jnp.float32),
        ),
        in_specs=[VMEM] * 6,
        out_specs=(VMEM, VMEM),
        compiler_params=small,
        name="products",
    )(own, up, down, self_term[None, :], residual, direction)
    shares = pl.pallas_call(
        spread_kernel,
        out_shape=jax.ShapeDtypeStruct((ring, 1, 4 * systems), jnp.float32),
        in_specs=[VMEM],
        out_specs=VMEM,
        compiler_params=small,
        name="spread",
    )(lax.all_to_all(shares, PLANE, 0, 0))
    return pl.pallas_call(
        update_kernel,
        out_shape=(jax.ShapeDtypeStruct((systems, block), jnp.float32),) * 3,
        in_specs=[VMEM] * 5,
        out_specs=(VMEM,) * 3,
        compiler_params=small,
        name="update",
    )(lax.all_to_all(shares, RING, 0, 0), solution, residual, direction, applied)


def solution(mesh):
    fine = Mesh(mesh.devices.reshape(SIZES), FINE)
    matrix = P(None, FINE)
    return jax.shard_map(
        on_device,
        mesh=fine,
        in_specs=(matrix, P(FINE), matrix, matrix, matrix),
        out_specs=(matrix, matrix, matrix),
        check_vma=False,
    )
```

```python
import functools
import math

import jax
import jax.numpy as jnp
from jax import lax
from jax.experimental import pallas as pl
from jax.experimental.pallas import tpu as pltpu
from jax.sharding import Mesh, PartitionSpec as P

FINE = ("x", "zl", "c", "y", "zh")
SIZES = (4, 2, 2, 4, 4)
RING = ("zl", "zh")
PLANE = ("x", "c", "y")
PART = 256
LANES = 1024
COORDS = 8
KERNEL_VMEM = 10 * 2**20
VMEM = pl.BlockSpec(memory_space=pltpu.VMEM)
SMEM = pl.BlockSpec(memory_space=pltpu.SMEM)


def shift(value, axes, by):
    size = lax.axis_size(axes)
    return lax.ppermute(value, axes, [(i, (i + by) % size) for i in range(size)])


def ring_shift(value, by):
    chips, half = lax.axis_size(RING), SIZES[4]
    place = lambda z, core: (z % 2) * 2 * half + core * half + z // 2
    hops = [(place(z, c), place((z + (1 - 2 * c) * by) % chips, c)) for z in range(chips) for c in range(2)]
    return lax.ppermute(value, ("zl", "c", "zh"), hops)


def pack_kernel(points, direction, mine, coords):
    systems = direction.shape[0]
    mine[...] = jnp.zeros_like(mine)
    mine[:systems, :] = direction[...]
    mine[systems : systems + 3, :] = points[...]
    coords[...] = jnp.broadcast_to(mine[systems:, :][None], coords.shape)


def prepare(groups, weights, rows):
    systems = weights.shape[0] // 2
    at = 0
    for group in groups:
        for b in range(group.shape[0]):
            block = group.shape[2]
            cols = slice(at, at + block)
            values = group[b, :systems, :]
            high = values.astype(jnp.bfloat16)
            weights[:systems, cols] = high
            weights[systems:, cols] = (values - high.astype(jnp.float32)).astype(jnp.bfloat16)
            for i in range(3):
                rows[8 * i : 8 * i + 8, cols] = jnp.broadcast_to(group[b, systems + i : systems + i + 1, :], (8, block))
            at += block


def accumulate(smoothing, wide, pairs, at, weights, rows, columns, out, tile_a, tile_b):
    systems = out.shape[1]

    def make(place, tile):
        first, column = place
        step = min(wide, LANES)
        for r in range(0, PART, 16):
            here = [jnp.broadcast_to(columns[pl.ds(first + r, 16), i : i + 1], (16, step)) for i in range(3)]
            for c in range(0, wide, step):
                lanes = pl.ds(column + c, step)
                far = [jnp.concatenate([rows[8 * i : 8 * i + 8, lanes]] * 2, axis=0) for i in range(3)]
                dx, dy, dz = (far[i] - here[i] for i in range(3))
                kernel = lax.rsqrt(dx * dx + dy * dy + (dz * dz + smoothing * smoothing))
                high = kernel.astype(jnp.bfloat16)
                low = (kernel - high.astype(jnp.float32)).astype(jnp.bfloat16)
                tile[r : r + 16, c : c + step] = high
                tile[PART + r : PART + r + 16, c : c + step] = low

    def multiply(place, tile):
        first, column = place
        product = lax.dot_general(
            tile[...],
            weights[:, pl.ds(column, wide)],
            (((1,), (1,)), ((), ())),
            preferred_element_type=jnp.float32,
        )
        out[pl.ds(first, PART), :] += (product[:PART, :systems] + product[PART:, systems:]) + (
            product[:PART, systems:] + product[PART:, :systems]
        )

    make(at(0, 0), tile_a)

    def two_steps(pair, carry):
        make(at(pair, 1), tile_b)
        multiply(at(pair, 0), tile_a)
        make(at(jnp.minimum(pair + 1, pairs - 1), 0), tile_a)
        multiply(at(pair, 1), tile_b)
        return carry

    lax.fori_loop(0, pairs, two_steps, 0)


def shard_at(z, offset, chips):
    z = lax.rem(z + offset, chips)
    return lax.rem(z, 2) * (chips // 2) + lax.div(z, 2)


def bulk_kernel(smoothing, wide, count, started, here, *refs):
    groups, refs = refs[:count], refs[count:]
    target, refs = refs[0], refs[1:]
    before, refs = (refs[0], refs[1:]) if started else (None, refs)
    out, weights, rows, columns, tile_a, tile_b = refs
    chips, _, block = target.shape
    for b in range(chips):
        columns[b * block : (b + 1) * block, :] = jnp.transpose(target[b])
    prepare(groups, weights, rows)
    out[...] = before[...] if started else jnp.zeros_like(out)

    def at(pair, half):
        shard = shard_at(here[0], pair + 1, chips) if started else pair
        return pl.multiple_of(shard * block, block), half * wide

    accumulate(smoothing, wide, chips - started, at, weights, rows, columns, out, tile_a, tile_b)


def step_kernel(smoothing, wide, offset, count, sets, arrived, here, *refs):
    groups, refs = refs[:count], refs[count:]
    prepared, refs = refs[: 2 * sets], refs[2 * sets :]
    target, before, refs = refs[0], refs[1], refs[2:]
    came, refs = (refs[0], refs[1:]) if arrived else (None, refs)
    out, refs = refs[0], refs[1:]
    if count:
        prepared, refs = refs[:2], refs[2:]
        prepare(groups, *prepared)
    columns, tile_a, tile_b = refs
    chips, _, block = target.shape
    which = shard_at(here[0], here[1] * offset + chips, chips)
    columns[...] = jnp.transpose(target[which])
    earlier = before[pl.ds(pl.multiple_of(which * block, block), block), :]
    out[...] = earlier + came[...] if arrived else earlier

    def at(pair, half):
        return 0, pl.multiple_of((2 * pair + half) * wide, wide)

    for i in range(0, len(prepared), 2):
        weights, rows = prepared[i : i + 2]
        pairs = weights.shape[1] // (2 * wide)
        accumulate(smoothing, wide, pairs, at, weights, rows, columns, out, tile_a, tile_b)


def cost(targets, sources, systems):
    return pl.CostEstimate(
        flops=16 * targets * sources * systems, bytes_accessed=4 * targets * systems, transcendentals=targets * sources
    )


def prepared_shapes(systems, sources):
    return [
        jax.ShapeDtypeStruct((2 * systems, sources), jnp.bfloat16),
        jax.ShapeDtypeStruct((24, sources), jnp.float32),
    ]


def bulk(here, groups, targets, before, smoothing):
    chips, coords, block = targets.shape
    systems = groups[0].shape[1] - coords
    sources = sum(g.shape[0] for g in groups) * block
    wide = sources // 2
    started = before is not None
    held = prepared_shapes(systems, sources)
    return pl.pallas_call(
        functools.partial(bulk_kernel, smoothing, wide, len(groups), started),
        out_shape=[jax.ShapeDtypeStruct((chips * block, systems), jnp.float32)] + (held if started else []),
        in_specs=[SMEM] + [VMEM] * (len(groups) + 1 + started),
        out_specs=[VMEM] * (3 if started else 1),
        scratch_shapes=([] if started else [pltpu.VMEM(h.shape, h.dtype) for h in held])
        + [
            pltpu.VMEM((chips * block, coords), jnp.float32),
            pltpu.VMEM((2 * PART, wide), jnp.bfloat16),
            pltpu.VMEM((2 * PART, wide), jnp.bfloat16),
        ],
        compiler_params=pltpu.CompilerParams(vmem_limit_bytes=KERNEL_VMEM),
        cost_estimate=cost(chips * block, sources, systems),
        name="bulk",
    )(here, *groups, targets, *([before] if started else []))


def ring_step(here, offset, groups, prepared, targets, before, arrived, smoothing, wide=512):
    chips, coords, block = targets.shape
    systems = before.shape[1]
    sources = sum(g.shape[0] for g in groups) * block + sum(p.shape[1] for p in prepared[::2])
    came = [] if arrived is None else [arrived]
    outs = [jax.ShapeDtypeStruct((block, systems), jnp.float32)]
    if groups:
        outs += prepared_shapes(systems, sources)
    operands = [*groups, *prepared, targets, before, *came]
    return pl.pallas_call(
        functools.partial(step_kernel, smoothing, wide, offset, len(groups), len(prepared) // 2, bool(came)),
        out_shape=outs,
        in_specs=[SMEM] + [VMEM] * len(operands),
        out_specs=[VMEM] * len(outs),
        scratch_shapes=[
            pltpu.VMEM((block, coords), jnp.float32),
            pltpu.VMEM((2 * PART, wide), jnp.bfloat16),
            pltpu.VMEM((2 * PART, wide), jnp.bfloat16),
        ],
        compiler_params=pltpu.CompilerParams(vmem_limit_bytes=KERNEL_VMEM),
        cost_estimate=cost(block, sources, systems),
        name="ring_step",
    )(here, *operands)


def column_sums(values):
    half = values.shape[1] // 2
    return jnp.sum(jnp.transpose(values[:, :half] + values[:, half:]), axis=0, keepdims=True)


def products_kernel(scale, own, up, down, self_term, residual_ref, direction_ref, applied_ref, sums_ref):
    total = (own[...] + up[...]) + down[...]
    direction = direction_ref[...]
    residual = residual_ref[...]
    applied = self_term[...] * direction + jnp.transpose(total) * scale
    applied_ref[...] = applied
    sums = jnp.concatenate(
        [
            column_sums(residual * residual),
            column_sums(direction * applied),
            column_sums(residual * applied),
            column_sums(applied * applied),
        ],
        axis=1,
    )
    sums_ref[...] = jnp.broadcast_to(sums[None], sums_ref.shape)


def spread_kernel(parts, out):
    out[...] = jnp.broadcast_to(jnp.sum(parts[...], axis=0, keepdims=True), out.shape)


def update_kernel(
    sums_ref, solution_ref, residual_ref, direction_ref, applied_ref, solution_out, residual_out, direction_out
):
    systems = solution_ref.shape[0]
    sums = jnp.sum(sums_ref[...], axis=0)
    norm_now, curvature, cross, image = (sums[:, i * systems : (i + 1) * systems] for i in range(4))
    step_len = norm_now / (curvature + 1e-06)
    norm_next = jnp.maximum(norm_now + step_len * (step_len * image - 2.0 * cross), 0.0)
    factor = norm_next / (norm_now + 1e-06)
    step_len = jnp.transpose(jnp.broadcast_to(step_len, (systems, systems)))
    factor = jnp.transpose(jnp.broadcast_to(factor, (systems, systems)))
    for c in range(0, solution_ref.shape[1], systems):
        cols = slice(c, c + systems)
        direction = direction_ref[:, cols]
        residual_next = residual_ref[:, cols] - step_len * applied_ref[:, cols]
        solution_out[:, cols] = solution_ref[:, cols] + step_len * direction
        residual_out[:, cols] = residual_next
        direction_out[:, cols] = residual_next + factor * direction


def on_device(points, self_term, solution, residual, direction):
    systems, block = direction.shape
    total = block * math.prod(SIZES)
    smoothing = 1.0 / math.sqrt(total)
    ring = lax.axis_size(RING)
    here = jnp.stack([lax.axis_index("zh") * 2 + lax.axis_index("zl"), 1 - 2 * lax.axis_index("c")])
    small = pltpu.CompilerParams(vmem_limit_bytes=16 * 2**20)

    mine, coords = pl.pallas_call(
        pack_kernel,
        out_shape=(
            jax.ShapeDtypeStruct((systems + COORDS, block), jnp.float32),
            jax.ShapeDtypeStruct((ring, COORDS, block), jnp.float32),
        ),
        in_specs=[VMEM] * 2,
        out_specs=(VMEM, VMEM),
        compiler_params=small,
        name="pack",
    )(points, direction)
    targets = lax.all_to_all(coords, RING, 0, 0)
    near = [shift(mine, "x", 1), shift(mine, "x", -1), shift(mine, "x", 2)]
    targets, *near[1:] = lax.optimization_barrier((targets, *near[1:]))
    line = jnp.stack([mine, *near])
    above, below = shift(line, "y", 1), shift(line, "y", -1)
    (sums,) = bulk(here, [line, shift(line, "c", 1)], targets, None, smoothing)
    sums, above, below = lax.optimization_barrier((sums, above, below))
    far = [shift(above[:2], "y", 1), shift(below[2:], "y", -1)]
    copies = [shift(above, "c", 1), shift(below, "c", 1)]
    sums, *second = bulk(here, [above, below], targets, sums, smoothing)
    sums, *far = lax.optimization_barrier((sums, *far))
    last = copies + far + [shift(part, "c", 1) for part in far]

    up, *third = ring_step(here, 4, last, [], targets, sums, None, smoothing)
    up = ring_shift(up, 1)
    (down,) = ring_step(here, -3, [], third, targets, sums, None, smoothing)
    down = ring_shift(down, -1)
    for away in (3, 2, 1):
        (up,) = ring_step(here, away, [], third, targets, sums, up, smoothing)
        up = ring_shift(up, 1)
        if away > 1:
            (down,) = ring_step(here, 1 - away, [], third, targets, sums, down, smoothing)
            down = ring_shift(down, -1)
    (own,) = ring_step(here, 0, [], second + third, targets, sums, None, smoothing)

    applied, shares = pl.pallas_call(
        functools.partial(products_kernel, 1.0 / math.sqrt(total)),
        out_shape=(
            jax.ShapeDtypeStruct((systems, block), jnp.float32),
            jax.ShapeDtypeStruct((lax.axis_size(PLANE), 1, 4 * systems), jnp.float32),
        ),
        in_specs=[VMEM] * 6,
        out_specs=(VMEM, VMEM),
        compiler_params=small,
        name="products",
    )(own, up, down, self_term[None, :], residual, direction)
    shares = pl.pallas_call(
        spread_kernel,
        out_shape=jax.ShapeDtypeStruct((ring, 1, 4 * systems), jnp.float32),
        in_specs=[VMEM],
        out_specs=VMEM,
        compiler_params=small,
        name="spread",
    )(lax.all_to_all(shares, PLANE, 0, 0))
    return pl.pallas_call(
        update_kernel,
        out_shape=(jax.ShapeDtypeStruct((systems, block), jnp.float32),) * 3,
        in_specs=[VMEM] * 5,
        out_specs=(VMEM,) * 3,
        compiler_params=small,
        name="update",
    )(lax.all_to_all(shares, RING, 0, 0), solution, residual, direction, applied)


def solution(mesh):
    fine = Mesh(mesh.devices.reshape(SIZES), FINE)
    matrix = P(None, FINE)
    return jax.shard_map(
        on_device,
        mesh=fine,
        in_specs=(matrix, P(FINE), matrix, matrix, matrix),
        out_specs=(matrix, matrix, matrix),
        check_vma=False,
    )
```

```python
import functools
import math

import jax
import jax.numpy as jnp
from jax import lax
from jax.experimental import pallas as pl
from jax.experimental.pallas import tpu as pltpu
from jax.sharding import Mesh, PartitionSpec as P

FINE = ("x", "zl", "c", "y", "zh")
SIZES = (4, 2, 2, 4, 4)
RING = ("zl", "zh")
PLANE = ("x", "c", "y")
PART = 256
LANES = 1024
COORDS = 8
KERNEL_VMEM = 10 * 2**20
VMEM = pl.BlockSpec(memory_space=pltpu.VMEM)
SMEM = pl.BlockSpec(memory_space=pltpu.SMEM)


def shift(value, axes, by):
    size = lax.axis_size(axes)
    return lax.ppermute(value, axes, [(i, (i + by) % size) for i in range(size)])


def ring_index(z):
    return (z % 2) * SIZES[4] + z // 2


def ring_shift(value, by):
    size = lax.axis_size(RING)
    return lax.ppermute(value, RING, [(ring_index(z), ring_index((z + by) % size)) for z in range(size)])


def pack_kernel(points, direction, mine, coords):
    systems = direction.shape[0]
    mine[...] = jnp.zeros_like(mine)
    mine[:systems, :] = direction[...]
    mine[systems : systems + 3, :] = points[...]
    coords[...] = jnp.broadcast_to(mine[systems:, :][None], coords.shape)


def prepare(groups, weights, rows):
    systems = weights.shape[0] // 2
    at = 0
    for group in groups:
        for b in range(group.shape[0]):
            block = group.shape[2]
            cols = slice(at, at + block)
            values = group[b, :systems, :]
            high = values.astype(jnp.bfloat16)
            weights[:systems, cols] = high
            weights[systems:, cols] = (values - high.astype(jnp.float32)).astype(jnp.bfloat16)
            for i in range(3):
                rows[8 * i : 8 * i + 8, cols] = jnp.broadcast_to(group[b, systems + i : systems + i + 1, :], (8, block))
            at += block


def accumulate(smoothing, wide, pairs, at, weights, rows, columns, out, tile_a, tile_b):
    systems = out.shape[1]

    def make(place, tile):
        first, column = place
        step = min(wide, LANES)
        for r in range(0, PART, 16):
            here = [jnp.broadcast_to(columns[pl.ds(first + r, 16), i : i + 1], (16, step)) for i in range(3)]
            for c in range(0, wide, step):
                lanes = pl.ds(column + c, step)
                far = [jnp.concatenate([rows[8 * i : 8 * i + 8, lanes]] * 2, axis=0) for i in range(3)]
                dx, dy, dz = (far[i] - here[i] for i in range(3))
                kernel = lax.rsqrt(dx * dx + dy * dy + (dz * dz + smoothing * smoothing))
                high = kernel.astype(jnp.bfloat16)
                low = (kernel - high.astype(jnp.float32)).astype(jnp.bfloat16)
                tile[r : r + 16, c : c + step] = high
                tile[PART + r : PART + r + 16, c : c + step] = low

    def multiply(place, tile):
        first, column = place
        product = lax.dot_general(
            tile[...],
            weights[:, pl.ds(column, wide)],
            (((1,), (1,)), ((), ())),
            preferred_element_type=jnp.float32,
        )
        out[pl.ds(first, PART), :] += (product[:PART, :systems] + product[PART:, systems:]) + (
            product[:PART, systems:] + product[PART:, :systems]
        )

    make(at(0, 0), tile_a)

    def two_steps(pair, carry):
        make(at(pair, 1), tile_b)
        multiply(at(pair, 0), tile_a)
        make(at(jnp.minimum(pair + 1, pairs - 1), 0), tile_a)
        multiply(at(pair, 1), tile_b)
        return carry

    lax.fori_loop(0, pairs, two_steps, 0)


def shard_at(z, offset, chips):
    z = lax.rem(z + offset, chips)
    return lax.rem(z, 2) * (chips // 2) + lax.div(z, 2)


def bulk_kernel(smoothing, wide, count, started, here, *refs):
    groups, refs = refs[:count], refs[count:]
    target, refs = refs[0], refs[1:]
    before, refs = (refs[0], refs[1:]) if started else (None, refs)
    out, weights, rows, columns, tile_a, tile_b = refs
    chips, _, block = target.shape
    for b in range(chips):
        columns[b * block : (b + 1) * block, :] = jnp.transpose(target[b])
    prepare(groups, weights, rows)
    out[...] = before[...] if started else jnp.zeros_like(out)

    def at(pair, half):
        if not started:
            return pl.multiple_of((2 * pair + half) * block, block), 0
        return pl.multiple_of(shard_at(here[0], pair + 1, chips) * block, block), half * wide

    accumulate(smoothing, wide, chips - 1 if started else chips // 2, at, weights, rows, columns, out, tile_a, tile_b)


def step_kernel(smoothing, wide, offset, count, sets, arrived, here, *refs):
    groups, refs = refs[:count], refs[count:]
    prepared, refs = refs[: 2 * sets], refs[2 * sets :]
    target, before, refs = refs[0], refs[1], refs[2:]
    came, refs = (refs[0], refs[1:]) if arrived else (None, refs)
    out, refs = refs[0], refs[1:]
    if count:
        prepared, refs = refs[:2], refs[2:]
        prepare(groups, *prepared)
    columns, tile_a, tile_b = refs
    chips, _, block = target.shape
    which = shard_at(here[0], offset, chips)
    columns[...] = jnp.transpose(target[which])
    earlier = before[pl.ds(pl.multiple_of(which * block, block), block), :]
    out[...] = earlier + came[...] if arrived else earlier

    def at(pair, half):
        return 0, pl.multiple_of((2 * pair + half) * wide, wide)

    for i in range(0, len(prepared), 2):
        weights, rows = prepared[i : i + 2]
        pairs = weights.shape[1] // (2 * wide)
        accumulate(smoothing, wide, pairs, at, weights, rows, columns, out, tile_a, tile_b)


def cost(targets, sources, systems):
    return pl.CostEstimate(
        flops=16 * targets * sources * systems, bytes_accessed=4 * targets * systems, transcendentals=targets * sources
    )


def prepared_shapes(systems, sources):
    return [
        jax.ShapeDtypeStruct((2 * systems, sources), jnp.bfloat16),
        jax.ShapeDtypeStruct((24, sources), jnp.float32),
    ]


def bulk(here, groups, targets, before, smoothing):
    chips, coords, block = targets.shape
    systems = groups[0].shape[1] - coords
    sources = sum(g.shape[0] for g in groups) * block
    started = before is not None
    wide = sources // 2 if started else sources
    held = prepared_shapes(systems, sources)
    return pl.pallas_call(
        functools.partial(bulk_kernel, smoothing, wide, len(groups), started),
        out_shape=[jax.ShapeDtypeStruct((chips * block, systems), jnp.float32)] + (held if started else []),
        in_specs=[SMEM] + [VMEM] * (len(groups) + 1 + started),
        out_specs=[VMEM] * (3 if started else 1),
        scratch_shapes=([] if started else [pltpu.VMEM(h.shape, h.dtype) for h in held])
        + [
            pltpu.VMEM((chips * block, coords), jnp.float32),
            pltpu.VMEM((2 * PART, wide), jnp.bfloat16),
            pltpu.VMEM((2 * PART, wide), jnp.bfloat16),
        ],
        compiler_params=pltpu.CompilerParams(vmem_limit_bytes=KERNEL_VMEM),
        cost_estimate=cost(chips * block, sources, systems),
        name="bulk",
    )(here, *groups, targets, *([before] if started else []))


def ring_step(here, offset, groups, prepared, targets, before, arrived, smoothing, wide=512):
    chips, coords, block = targets.shape
    systems = before.shape[1]
    sources = sum(g.shape[0] for g in groups) * block + sum(p.shape[1] for p in prepared[::2])
    came = [] if arrived is None else [arrived]
    outs = [jax.ShapeDtypeStruct((block, systems), jnp.float32)]
    if groups:
        outs += prepared_shapes(systems, sources)
    operands = [*groups, *prepared, targets, before, *came]
    return pl.pallas_call(
        functools.partial(step_kernel, smoothing, wide, offset % chips, len(groups), len(prepared) // 2, bool(came)),
        out_shape=outs,
        in_specs=[SMEM] + [VMEM] * len(operands),
        out_specs=[VMEM] * len(outs),
        scratch_shapes=[
            pltpu.VMEM((block, coords), jnp.float32),
            pltpu.VMEM((2 * PART, wide), jnp.bfloat16),
            pltpu.VMEM((2 * PART, wide), jnp.bfloat16),
        ],
        compiler_params=pltpu.CompilerParams(vmem_limit_bytes=KERNEL_VMEM),
        cost_estimate=cost(block, sources, systems),
        name="ring_step",
    )(here, *operands)


def column_sums(values):
    half = values.shape[1] // 2
    return jnp.sum(jnp.transpose(values[:, :half] + values[:, half:]), axis=0, keepdims=True)


def products_kernel(scale, own, up, down, self_term, residual_ref, direction_ref, applied_ref, sums_ref):
    total = (own[...] + up[...]) + down[...]
    direction = direction_ref[...]
    residual = residual_ref[...]
    applied = self_term[...] * direction + jnp.transpose(total) * scale
    applied_ref[...] = applied
    sums = jnp.concatenate(
        [
            column_sums(residual * residual),
            column_sums(direction * applied),
            column_sums(residual * applied),
            column_sums(applied * applied),
        ],
        axis=1,
    )
    sums_ref[...] = jnp.broadcast_to(sums[None], sums_ref.shape)


def spread_kernel(parts, out):
    out[...] = jnp.broadcast_to(jnp.sum(parts[...], axis=0, keepdims=True), out.shape)


def update_kernel(
    sums_ref, solution_ref, residual_ref, direction_ref, applied_ref, solution_out, residual_out, direction_out
):
    systems = solution_ref.shape[0]
    sums = jnp.sum(sums_ref[...], axis=0)
    norm_now, curvature, cross, image = (sums[:, i * systems : (i + 1) * systems] for i in range(4))
    step_len = norm_now / (curvature + 1e-06)
    norm_next = jnp.maximum(norm_now + step_len * (step_len * image - 2.0 * cross), 0.0)
    factor = norm_next / (norm_now + 1e-06)
    step_len = jnp.transpose(jnp.broadcast_to(step_len, (systems, systems)))
    factor = jnp.transpose(jnp.broadcast_to(factor, (systems, systems)))
    for c in range(0, solution_ref.shape[1], systems):
        cols = slice(c, c + systems)
        direction = direction_ref[:, cols]
        residual_next = residual_ref[:, cols] - step_len * applied_ref[:, cols]
        solution_out[:, cols] = solution_ref[:, cols] + step_len * direction
        residual_out[:, cols] = residual_next
        direction_out[:, cols] = residual_next + factor * direction


def on_device(points, self_term, solution, residual, direction):
    systems, block = direction.shape
    total = block * math.prod(SIZES)
    smoothing = 1.0 / math.sqrt(total)
    ring = lax.axis_size(RING)
    here = jnp.reshape(lax.axis_index("zh") * 2 + lax.axis_index("zl"), (1,))
    small = pltpu.CompilerParams(vmem_limit_bytes=16 * 2**20)

    mine, coords = pl.pallas_call(
        pack_kernel,
        out_shape=(
            jax.ShapeDtypeStruct((systems + COORDS, block), jnp.float32),
            jax.ShapeDtypeStruct((ring, COORDS, block), jnp.float32),
        ),
        in_specs=[VMEM] * 2,
        out_specs=(VMEM, VMEM),
        compiler_params=small,
        name="pack",
    )(points, direction)
    targets = lax.all_to_all(coords, RING, 0, 0)
    near = [shift(mine, "x", 1), shift(mine, "x", -1), shift(mine, "x", 2)]
    targets, *near[1:] = lax.optimization_barrier((targets, *near[1:]))
    line = jnp.stack([mine, *near])
    above, below = shift(line, "y", 1), shift(line, "y", -1)
    (sums,) = bulk(here, [line, shift(line, "c", 1)], targets, None, smoothing)
    sums, above, below = lax.optimization_barrier((sums, above, below))
    far = [shift(above[:2], "y", 1), shift(below[2:], "y", -1)]
    copies = [shift(above, "c", 1), shift(below, "c", 1)]
    sums, *second = bulk(here, [above, below], targets, sums, smoothing)
    sums, *far = lax.optimization_barrier((sums, *far))
    last = copies + far + [shift(part, "c", 1) for part in far]

    up, *third = ring_step(here, 4, last, [], targets, sums, None, smoothing)
    up = ring_shift(up, 1)
    (down,) = ring_step(here, -3, [], third, targets, sums, None, smoothing)
    down = ring_shift(down, -1)
    for away in (3, 2, 1):
        (up,) = ring_step(here, away, [], third, targets, sums, up, smoothing)
        up = ring_shift(up, 1)
        if away > 1:
            (down,) = ring_step(here, 1 - away, [], third, targets, sums, down, smoothing)
            down = ring_shift(down, -1)
    (own,) = ring_step(here, 0, [], second + third, targets, sums, None, smoothing)

    applied, shares = pl.pallas_call(
        functools.partial(products_kernel, 1.0 / math.sqrt(total)),
        out_shape=(
            jax.ShapeDtypeStruct((systems, block), jnp.float32),
            jax.ShapeDtypeStruct((lax.axis_size(PLANE), 1, 4 * systems), jnp.float32),
        ),
        in_specs=[VMEM] * 6,
        out_specs=(VMEM, VMEM),
        compiler_params=small,
        name="products",
    )(own, up, down, self_term[None, :], residual, direction)
    shares = pl.pallas_call(
        spread_kernel,
        out_shape=jax.ShapeDtypeStruct((ring, 1, 4 * systems), jnp.float32),
        in_specs=[VMEM],
        out_specs=VMEM,
        compiler_params=small,
        name="spread",
    )(lax.all_to_all(shares, PLANE, 0, 0))
    return pl.pallas_call(
        update_kernel,
        out_shape=(jax.ShapeDtypeStruct((systems, block), jnp.float32),) * 3,
        in_specs=[VMEM] * 5,
        out_specs=(VMEM,) * 3,
        compiler_params=small,
        name="update",
    )(lax.all_to_all(shares, RING, 0, 0), solution, residual, direction, applied)


def solution(mesh):
    fine = Mesh(mesh.devices.reshape(SIZES), FINE)
    matrix = P(None, FINE)
    return jax.shard_map(
        on_device,
        mesh=fine,
        in_specs=(matrix, P(FINE), matrix, matrix, matrix),
        out_specs=(matrix, matrix, matrix),
        check_vma=False,
    )
```
